512 devices in a mesh: row: 32 (over z_lo, x), col: 16 (over z_hi, y, core).
Axes of the slice: x: 4, y: 4, z: 16 (z_hi: 2, z_lo: 8; z = z_hi * 8 + z_lo), core: 2. Of those that a mesh axis runs over, the one named last changes fastest.
Arguments:
- amplitudes: bfloat16 [12, 1024, 1024], P(None, 'row', 'col'), may hold values from -6 to 6
- cycle_vertex: bfloat16 [12, 1024, 1024], P(None, 'row', 'col'), may hold values from -0.1875 to 0.1875
- occupied_irrep: int32 [12], replicated, may hold values from 0 to 7
- virtual_irrep: int32 [1024], replicated, may hold values from 0 to 7
Outputs:
- residual: bfloat16 [12, 1024, 12288], P(None, 'row', 'col')
The draws below stay inside these ranges and needn't reach their ends.
Inputs may be any that keep to these rules, and one draw needn't show every extreme that they name: `occupied_irrep`: D2h irrep labels; the product of two irreps is the bitwise exclusive or of their labels. `virtual_irrep`: D2h irrep labels; the product of two irreps is the bitwise exclusive or of their labels.
All inputs are finite; a program needn't handle non-finite values.
Results may differ from the reference program's by a relative error of at most 0.01.
Values may be sent and summed in bfloat16 or wider, within the bound.
No kernel may reach another device: no remote copies, remote signals or barrier semaphores. Data moves between devices by JAX's collectives and lax.ppermute only.
A program may use at most 64 MiB of HBM per device.

```python
import jax
import jax.numpy as jnp
from jax import lax

V = 1024
O = 12


def plant(values, key, low, high):
    longest = values.shape.index(max(values.shape))
    spots = []
    for shift in (0, 1):
        where = [jax.random.randint(jax.random.fold_in(key, axis), (), 0, length) for axis, length in enumerate(values.shape)]
        where[longest] = (where[longest] + shift) % values.shape[longest]
        spots.append(tuple(where))
    return values.at[spots[0]].set(low).at[spots[1]].set(high)


def level_of(stream_key, extent, shards, smallest, top_value):
    gain, own = 1.0, jax.random.fold_in(stream_key, 6)
    for axis_at, blocks in shards:
        heights = jnp.exp(jax.random.uniform(jax.random.fold_in(own, axis_at), (blocks,), jnp.float32, smallest / len(shards), top_value / len(shards)))
        gain = gain * jnp.repeat(heights, extent[axis_at] // blocks).reshape([-1 if axis == axis_at else 1 for axis in range(len(extent))])
    return gain


def normal_values(rng, dims, width, reach, split=(), dtype=jnp.bfloat16):
    entries = jax.random.normal(rng, dims, jnp.float32) * width
    if len(split) > 0:
        entries = level_of(rng, dims, split, -0.22, 0.18) * entries
    return jnp.clip(entries, min=-reach, max=reach).astype(dtype)


def setup_inputs(seed: int = 0) -> dict:
    key_list = jax.random.split(jax.random.key(seed), 5)
    return {
        "amplitudes": normal_values(key_list[0], (O, V, V), 1.0, 6.0, ((1, 32), (2, 16))),
        "cycle_vertex": normal_values(key_list[1], (O, V, V), V ** -0.5, 0.1875, ((1, 32), (2, 16))),
        "occupied_irrep": plant(jax.random.randint(key_list[2], (O,), 0, 8), jax.random.fold_in(key_list[2], 1), 0, 7).astype(jnp.int32),
        "virtual_irrep": plant(jax.random.randint(key_list[3], (V,), 0, 8), jax.random.fold_in(key_list[3], 1), 0, 7).astype(jnp.int32),
    }


def reference(amplitudes, cycle_vertex, occupied_irrep, virtual_irrep):
    amp_float = amplitudes.astype(jnp.float32)
    vertex_float = cycle_vertex.astype(jnp.float32)
    occ_count = amplitudes.shape[0]
    virt_count = amplitudes.shape[1]

    def per_row(position):
        amp_row = lax.dynamic_index_in_dim(amp_float, position, 0, keepdims=False)
        vertex_row = lax.dynamic_index_in_dim(vertex_float, position, 0, keepdims=False)
        direct = jnp.einsum("ac,jcb->abj", amp_row, vertex_float, precision=lax.Precision.HIGHEST)
        crossed = jnp.einsum("jac,cb->abj", amp_float, vertex_row, precision=lax.Precision.HIGHEST)
        paired = lax.optimization_barrier((direct - crossed).astype(jnp.bfloat16)).astype(jnp.float32)
        own_irrep = lax.dynamic_index_in_dim(occupied_irrep, position, 0, keepdims=False)
        product_irrep = jnp.bitwise_xor(own_irrep, occupied_irrep[None, None, :])
        product_irrep = jnp.bitwise_xor(product_irrep, virtual_irrep[:, None, None])
        product_irrep = jnp.bitwise_xor(product_irrep, virtual_irrep[None, :, None])
        allowed = (product_irrep == 0).astype(jnp.float32)
        result = (allowed * (paired - jnp.swapaxes(paired, 0, 1))).astype(jnp.bfloat16)
        return result.reshape(virt_count, virt_count * occ_count)

    return lax.map(per_row, jnp.arange(occ_count).astype(jnp.int32))
```

```python
import functools

import jax
import jax.numpy as jnp
from jax import lax
from jax.experimental import pallas as pl
from jax.experimental.pallas import tpu as pltpu
from jax.sharding import PartitionSpec as P

Z, X, H, YC = 8, 4, 2, 8
OCC, WA, WB = 12, 32, 64
HALF = 32
GROUPS = OCC // 4
SIDE = OCC * 32
TILES = 17
VMEM_LIMIT = 48 * 1024 * 1024


def z_groups():
    return [[z * X + x for z in range(Z)] for x in range(X)]


def x_groups():
    return [[z * X + x for x in range(X)] for z in range(Z)]


def yc_groups():
    return [[h * YC + k for k in range(YC)] for h in range(H)]


def h_swap():
    return [(h * YC + k, (1 - h) * YC + k) for h in range(H) for k in range(YC)]


def mirror_perm(step):
    rows, cols = Z * X, H * YC
    return [
        (r * cols + c, (2 * c + (step + r) % 2) * cols + r // 2)
        for r in range(rows)
        for c in range(cols)
    ]


def slot_of(shape):
    return lax.broadcasted_iota(jnp.int32, shape, 1) // HALF


def crossed(load, i, group):
    slot = slot_of((32, 128))
    out = None
    for s in range(4):
        piece = load(4 * group + s, i // 4)
        shift = (s - i % 4) % 4
        if shift:
            piece = pltpu.roll(piece, shift * HALF, 1)
        out = piece if out is None else jnp.where(slot == s, piece, out)
    return out


def full_tiles():
    return [(i, g) for i in range(OCC) for g in range(i // 4 + 1, GROUPS)]


def pack_kernel(a_ref, w_ref, a_out, w_out):
    for i in range(OCC // 2):
        a_out[32 * i : 32 * i + 32, :] = jnp.concatenate([a_ref[i], a_ref[i + 6]], axis=1)
    for g in range(GROUPS):
        block = [w_ref[4 * g + s].astype(jnp.float32) for s in range(4)]
        for half in range(2):
            cut = jnp.concatenate(
                [b[:, HALF * half : HALF * half + HALF] for b in block], axis=1
            ).astype(jnp.bfloat16)
            lane = half * SIDE + 128 * g
            for copy in range(Z):
                w_out[copy, :, lane : lane + 128] = cut


def pack(amplitudes, cycle_vertex):
    return pl.pallas_call(
        pack_kernel,
        out_shape=(
            jax.ShapeDtypeStruct((192, 128), jnp.bfloat16),
            jax.ShapeDtypeStruct((Z, 32, 2 * SIDE), jnp.bfloat16),
        ),
        compiler_params=pltpu.CompilerParams(vmem_limit_bytes=VMEM_LIMIT),
        name="pack",
    )(amplitudes, cycle_vertex)


def pair_kernel(row_ref, a_ref, w_ref, paired_ref, send0_ref, send1_ref, w_own, lhs, prod, turned, sem):
    copies = [pltpu.make_async_copy(w_ref.at[x], w_own.at[:, x], sem.at[x]) for x in range(X)]
    for copy in copies:
        copy.start()
    for z in range(Z):
        h, y = z // 4, z % 4
        first = a_ref[2 * y, h]
        second = a_ref[2 * y + 1, h]
        lhs[:192, 128 * z : 128 * z + 128] = jnp.concatenate([first[:, :64], second[:, :64]], axis=1)
        lhs[192:, 128 * z : 128 * z + 128] = jnp.concatenate([first[:, 64:], second[:, 64:]], axis=1)
    for copy in copies:
        copy.wait()
    prod[...] = jnp.dot(
        lhs[...], w_own[...].reshape(Z * X * 32, 2 * SIDE), preferred_element_type=jnp.float32
    )
    slot = slot_of((32, 128))
    flip = row_ref[0]
    for half in range(2):
        lane = half * SIDE

        def load(j, group):
            return prod[32 * j : 32 * j + 32, lane + 128 * group : lane + 128 * group + 128]

        for i in range(OCC):
            for g in range(GROUPS):
                paired_ref[half, 32 * i : 32 * i + 32, 128 * g : 128 * g + 128] = (
                    load(i, g) - crossed(load, i, g)
                ).astype(jnp.bfloat16)
        turned[...] = paired_ref[half].astype(jnp.float32).T

        def tile(i, group):
            return turned[32 * i : 32 * i + 32, 128 * group : 128 * group + 128]

        out = [tile(i, g) for i, g in full_tiles()]
        for q in range(GROUPS):
            out.append(jnp.where(slot == 0, pltpu.roll(tile(4 * q + 2, q), HALF, 1), tile(4 * q, q)))
        out.append(jnp.where(slot < 2, pltpu.roll(tile(5, 1), 2 * HALF, 1), tile(1, 0)))
        out.append(tile(9, 2))
        packed = jnp.concatenate(out, axis=0).astype(jnp.bfloat16)

        @pl.when(flip == half)
        def _():
            send0_ref[...] = packed

        @pl.when(flip != half)
        def _():
            send1_ref[...] = packed


def pair(row, a_all, w_all):
    vmem = pl.BlockSpec(memory_space=pltpu.VMEM)
    send = jax.ShapeDtypeStruct((TILES * 32, 128), jnp.bfloat16)
    return pl.pallas_call(
        pair_kernel,
        out_shape=(jax.ShapeDtypeStruct((2, SIDE, SIDE), jnp.bfloat16), send, send),
        in_specs=[pl.BlockSpec(memory_space=pltpu.SMEM), vmem, pl.BlockSpec(memory_space=pl.ANY)],
        out_specs=(vmem, vmem, vmem),
        scratch_shapes=[
            pltpu.VMEM((Z, X, 32, 2 * SIDE), jnp.bfloat16),
            pltpu.VMEM((SIDE, Z * 128), jnp.bfloat16),
            pltpu.VMEM((SIDE, 2 * SIDE), jnp.float32),
            pltpu.VMEM((SIDE, SIDE), jnp.float32),
            pltpu.SemaphoreType.DMA((X,)),
        ],
        compiler_params=pltpu.CompilerParams(vmem_limit_bytes=VMEM_LIMIT),
        name="pair",
    )(row, a_all, w_all)


def finish_kernel(row_ref, paired_ref, get0_ref, get1_ref, row_key, col_key, order, out_ref, upper, whole):
    slot = slot_of((32, 128))
    flip = row_ref[0]
    for half in range(2):
        def got(t):
            rows = slice(32 * t, 32 * t + 32)
            return jnp.where(flip == half, get0_ref[rows, :], get1_ref[rows, :]).astype(jnp.float32)

        def put(i, group, mirrored, floor):
            rows, lanes = slice(32 * i, 32 * i + 32), slice(128 * group, 128 * group + 128)
            diff = paired_ref[half, rows, lanes].astype(jnp.float32) + mirrored
            if floor >= 0:
                diff = jnp.where(slot > floor, diff, 0.0)
            upper[rows, lanes] = diff

        for t, (i, g) in enumerate(full_tiles()):
            put(i, g, got(t), -1)
        last = [got(15), got(16)]
        for q in range(GROUPS):
            piece = got(12 + q)
            put(4 * q, q, piece, 0)
            put(4 * q + 2, q, pltpu.roll(piece, 3 * HALF, 1), 2)
            put(4 * q + 1, q, (last[0], pltpu.roll(last[0], 2 * HALF, 1), last[1])[q], 1)
            upper[32 * (4 * q + 3) : 32 * (4 * q + 4), 128 * q : 128 * q + 128] = jnp.zeros((32, 128), jnp.float32)

        def load(j, group):
            return upper[32 * j : 32 * j + 32, 128 * group : 128 * group + 128]

        for i in range(OCC):
            rows = slice(32 * i, 32 * i + 32)
            for g in range(GROUPS):
                lanes = slice(128 * g, 128 * g + 128)
                if g > i // 4:
                    value = load(i, g)
                elif g < i // 4:
                    value = -crossed(load, i, g)
                else:
                    value = load(i, g) - crossed(load, i, g)
                allowed = row_key[rows, :] == col_key[half : half + 1, lanes]
                whole[rows, lanes] = jnp.where(allowed, value, 0.0).astype(jnp.bfloat16)
        out_ref[:, SIDE * half : SIDE * half + SIDE] = jnp.dot(
            whole[...], order[...], preferred_element_type=jnp.float32
        ).astype(jnp.bfloat16)


def finish(row, paired, get0, get1, row_key, col_key, order):
    vmem = pl.BlockSpec(memory_space=pltpu.VMEM)
    return pl.pallas_call(
        finish_kernel,
        out_shape=jax.ShapeDtypeStruct((SIDE, 2 * SIDE), jnp.bfloat16),
        in_specs=[pl.BlockSpec(memory_space=pltpu.SMEM)] + [vmem] * 6,
        out_specs=vmem,
        scratch_shapes=[
            pltpu.VMEM((SIDE, SIDE), jnp.float32),
            pltpu.VMEM((SIDE, SIDE), jnp.bfloat16),
        ],
        compiler_params=pltpu.CompilerParams(vmem_limit_bytes=VMEM_LIMIT),
        name="finish",
    )(row, paired, get0, get1, row_key, col_key, order)


def on_device(amplitudes, cycle_vertex, occupied_irrep, virtual_irrep):
    r, c = lax.axis_index("row"), lax.axis_index("col")
    flip = (r % 2).astype(jnp.int32).reshape(1)
    a_own, w_own = pack(amplitudes, cycle_vertex)
    w_z = lax.all_to_all(w_own, "row", 0, 0, tiled=True, axis_index_groups=z_groups())
    w_all = lax.all_to_all(
        jnp.broadcast_to(w_z[None], (X, Z, 32, 2 * SIDE)),
        "row", 0, 0, tiled=True, axis_index_groups=x_groups(),
    )
    a_far = lax.ppermute(a_own, "col", h_swap())
    low = c < YC
    a_two = jnp.stack([jnp.where(low, a_own, a_far), jnp.where(low, a_far, a_own)])
    a_all = lax.all_to_all(
        jnp.broadcast_to(a_two[None], (YC, H, 192, 128)),
        "col", 0, 0, tiled=True, axis_index_groups=yc_groups(),
    )
    paired, send0, send1 = pair(flip, a_all, w_all)
    get0 = lax.ppermute(send0, ("row", "col"), mirror_perm(0))
    get1 = lax.ppermute(send1, ("row", "col"), mirror_perm(1))
    irrep_a = lax.dynamic_slice_in_dim(virtual_irrep, r * WA, WA)
    irrep_b = lax.dynamic_slice_in_dim(virtual_irrep, c * WB, WB)
    row_key = (occupied_irrep[:, None] ^ irrep_a[None, :]).reshape(SIDE, 1)
    row_key = jnp.broadcast_to(row_key, (SIDE, 128))
    col_key = (occupied_irrep[None, :, None] ^ irrep_b.reshape(2, 1, HALF)).reshape(2, SIDE)
    source = jnp.arange(SIDE)
    order = ((source % HALF) * OCC + source // HALF)[:, None] == jnp.arange(SIDE)[None, :]
    result = finish(flip, paired, get0, get1, row_key, col_key, order.astype(jnp.bfloat16))
    return result.reshape(OCC, WA, WB * OCC)


def solution(mesh):
    return jax.shard_map(
        on_device,
        mesh=mesh,
        in_specs=(P(None, "row", "col"), P(None, "row", "col"), P(), P()),
        out_specs=P(None, "row", "col"),
        check_vma=False,
    )
```

```python
import functools

import jax
import jax.numpy as jnp
from jax import lax
from jax.experimental import pallas as pl
from jax.experimental.pallas import tpu as pltpu
from jax.sharding import PartitionSpec as P

Z, X, H, YC = 8, 4, 2, 8
OCC, WA, WB = 12, 32, 64
HALF = 32
GROUPS = OCC // 4
SIDE = OCC * 32
TILES = 17
VMEM_LIMIT = 48 * 1024 * 1024


def z_groups():
    return [[z * X + x for z in range(Z)] for x in range(X)]


def x_groups():
    return [[z * X + x for x in range(X)] for z in range(Z)]


def yc_groups():
    return [[h * YC + k for k in range(YC)] for h in range(H)]


def h_swap():
    return [(h * YC + k, (1 - h) * YC + k) for h in range(H) for k in range(YC)]


def y_shift(step):
    return [
        (h * YC + y * 2 + k, h * YC + (y + step) % 4 * 2 + k)
        for h in range(H) for y in range(4) for k in range(2)
    ]


def core_swap():
    return [(c, c ^ 1) for c in range(H * YC)]


def mirror_perm(step):
    rows, cols = Z * X, H * YC
    return [
        (r * cols + c, (2 * c + (step + r) % 2) * cols + r // 2)
        for r in range(rows)
        for c in range(cols)
    ]


def slot_of(shape):
    return lax.broadcasted_iota(jnp.int32, shape, 1) // HALF


def crossed(load, i, group):
    slot = slot_of((32, 128))
    out = None
    for s in range(4):
        piece = load(4 * group + s, i // 4)
        shift = (s - i % 4) % 4
        if shift:
            piece = pltpu.roll(piece, shift * HALF, 1)
        out = piece if out is None else jnp.where(slot == s, piece, out)
    return out


def full_tiles():
    return [(i, g) for i in range(OCC) for g in range(i // 4 + 1, GROUPS)]


def pack_kernel(a_ref, w_ref, a_out, w_out):
    for i in range(OCC // 2):
        a_out[32 * i : 32 * i + 32, :] = jnp.concatenate([a_ref[i], a_ref[i + 6]], axis=1)
    for g in range(GROUPS):
        block = [w_ref[4 * g + s].astype(jnp.float32) for s in range(4)]
        for half in range(2):
            cut = jnp.concatenate(
                [b[:, HALF * half : HALF * half + HALF] for b in block], axis=1
            ).astype(jnp.bfloat16)
            lane = half * SIDE + 128 * g
            for copy in range(Z):
                w_out[copy, :, lane : lane + 128] = cut


def pack(amplitudes, cycle_vertex):
    return pl.pallas_call(
        pack_kernel,
        out_shape=(
            jax.ShapeDtypeStruct((192, 128), jnp.bfloat16),
            jax.ShapeDtypeStruct((Z, 32, 2 * SIDE), jnp.bfloat16),
        ),
        compiler_params=pltpu.CompilerParams(vmem_limit_bytes=VMEM_LIMIT),
        name="pack",
    )(amplitudes, cycle_vertex)


def pair_kernel(row_ref, own_ref, far_ref, w_ref, paired_ref, send0_ref, send1_ref, w_own, lhs, prod, turned, sem):
    copies = [pltpu.make_async_copy(w_ref.at[x], w_own.at[:, x], sem.at[x]) for x in range(X)]
    for copy in copies:
        copy.start()
    core, y = row_ref[1], row_ref[2]
    for step in range(4):
        for h in range(H):
            mine, other = own_ref[step, h], far_ref[step, h]
            first = jnp.where(core == 0, mine, other)
            second = jnp.where(core == 0, other, mine)
            z = h * 4 + lax.rem(y + 4 - step, 4)
            lhs[z, :192] = jnp.concatenate([first[:, :64], second[:, :64]], axis=1)
            lhs[z, 192:] = jnp.concatenate([first[:, 64:], second[:, 64:]], axis=1)
    for copy in copies:
        copy.wait()
    prod[...] = jnp.dot(
        jnp.concatenate([lhs[z] for z in range(Z)], axis=1), w_own[...].reshape(Z * X * 32, 2 * SIDE), preferred_element_type=jnp.float32
    )
    slot = slot_of((32, 128))
    flip = row_ref[0]
    for half in range(2):
        lane = half * SIDE

        def load(j, group):
            return prod[32 * j : 32 * j + 32, lane + 128 * group : lane + 128 * group + 128]

        for i in range(OCC):
            for g in range(GROUPS):
                paired_ref[half, 32 * i : 32 * i + 32, 128 * g : 128 * g + 128] = (
                    load(i, g) - crossed(load, i, g)
                ).astype(jnp.bfloat16)
        turned[...] = paired_ref[half].astype(jnp.float32).T

        def tile(i, group):
            return turned[32 * i : 32 * i + 32, 128 * group : 128 * group + 128]

        out = [tile(i, g) for i, g in full_tiles()]
        for q in range(GROUPS):
            out.append(jnp.where(slot == 0, pltpu.roll(tile(4 * q + 2, q), HALF, 1), tile(4 * q, q)))
        out.append(jnp.where(slot < 2, pltpu.roll(tile(5, 1), 2 * HALF, 1), tile(1, 0)))
        out.append(tile(9, 2))
        packed = jnp.concatenate(out, axis=0).astype(jnp.bfloat16)

        @pl.when(flip == half)
        def _():
            send0_ref[...] = packed

        @pl.when(flip != half)
        def _():
            send1_ref[...] = packed


def pair(row, a_mine, a_other, w_all):
    vmem = pl.BlockSpec(memory_space=pltpu.VMEM)
    send = jax.ShapeDtypeStruct((TILES * 32, 128), jnp.bfloat16)
    return pl.pallas_call(
        pair_kernel,
        out_shape=(jax.ShapeDtypeStruct((2, SIDE, SIDE), jnp.bfloat16), send, send),
        in_specs=[pl.BlockSpec(memory_space=pltpu.SMEM), vmem, vmem, pl.BlockSpec(memory_space=pl.ANY)],
        out_specs=(vmem, vmem, vmem),
        scratch_shapes=[
            pltpu.VMEM((Z, X, 32, 2 * SIDE), jnp.bfloat16),
            pltpu.VMEM((Z, SIDE, 128), jnp.bfloat16),
            pltpu.VMEM((SIDE, 2 * SIDE), jnp.float32),
            pltpu.VMEM((SIDE, SIDE), jnp.float32),
            pltpu.SemaphoreType.DMA((X,)),
        ],
        compiler_params=pltpu.CompilerParams(vmem_limit_bytes=VMEM_LIMIT),
        name="pair",
    )(row, a_mine, a_other, w_all)


def finish_kernel(row_ref, paired_ref, get0_ref, get1_ref, row_key, col_key, order, out_ref, upper, whole):
    slot = slot_of((32, 128))
    flip = row_ref[0]
    for half in range(2):
        def got(t):
            rows = slice(32 * t, 32 * t + 32)
            return jnp.where(flip == half, get0_ref[rows, :], get1_ref[rows, :]).astype(jnp.float32)

        def put(i, group, mirrored, floor):
            rows, lanes = slice(32 * i, 32 * i + 32), slice(128 * group, 128 * group + 128)
            diff = paired_ref[half, rows, lanes].astype(jnp.float32) + mirrored
            if floor >= 0:
                diff = jnp.where(slot > floor, diff, 0.0)
            upper[rows, lanes] = diff

        for t, (i, g) in enumerate(full_tiles()):
            put(i, g, got(t), -1)
        last = [got(15), got(16)]
        for q in range(GROUPS):
            piece = got(12 + q)
            put(4 * q, q, piece, 0)
            put(4 * q + 2, q, pltpu.roll(piece, 3 * HALF, 1), 2)
            put(4 * q + 1, q, (last[0], pltpu.roll(last[0], 2 * HALF, 1), last[1])[q], 1)
            upper[32 * (4 * q + 3) : 32 * (4 * q + 4), 128 * q : 128 * q + 128] = jnp.zeros((32, 128), jnp.float32)

        def load(j, group):
            return upper[32 * j : 32 * j + 32, 128 * group : 128 * group + 128]

        for i in range(OCC):
            rows = slice(32 * i, 32 * i + 32)
            for g in range(GROUPS):
                lanes = slice(128 * g, 128 * g + 128)
                if g > i // 4:
                    value = load(i, g)
                elif g < i // 4:
                    value = -crossed(load, i, g)
                else:
                    value = load(i, g) - crossed(load, i, g)
                allowed = row_key[rows, :] == col_key[half : half + 1, lanes]
                whole[rows, lanes] = jnp.where(allowed, value, 0.0).astype(jnp.bfloat16)
        out_ref[:, SIDE * half : SIDE * half + SIDE] = jnp.dot(
            whole[...], order[...], preferred_element_type=jnp.float32
        ).astype(jnp.bfloat16)


def finish(row, paired, get0, get1, row_key, col_key, order):
    vmem = pl.BlockSpec(memory_space=pltpu.VMEM)
    return pl.pallas_call(
        finish_kernel,
        out_shape=jax.ShapeDtypeStruct((SIDE, 2 * SIDE), jnp.bfloat16),
        in_specs=[pl.BlockSpec(memory_space=pltpu.SMEM)] + [vmem] * 6,
        out_specs=vmem,
        scratch_shapes=[
            pltpu.VMEM((SIDE, SIDE), jnp.float32),
            pltpu.VMEM((SIDE, SIDE), jnp.bfloat16),
        ],
        compiler_params=pltpu.CompilerParams(vmem_limit_bytes=VMEM_LIMIT),
        name="finish",
    )(row, paired, get0, get1, row_key, col_key, order)


def on_device(amplitudes, cycle_vertex, occupied_irrep, virtual_irrep):
    r, c = lax.axis_index("row"), lax.axis_index("col")
    place = jnp.stack([r % 2, c % 2, c // 2 % 4]).astype(jnp.int32)
    a_own, w_own = pack(amplitudes, cycle_vertex)
    w_z = lax.all_to_all(w_own, "row", 0, 0, tiled=True, axis_index_groups=z_groups())
    a_far = lax.ppermute(a_own, "col", h_swap())
    low = c < YC
    a_two = jnp.stack([jnp.where(low, a_own, a_far), jnp.where(low, a_far, a_own)])
    w_z, a_two = lax.optimization_barrier((w_z, a_two))
    w_all = lax.all_to_all(
        jnp.broadcast_to(w_z[None], (X, Z, 32, 2 * SIDE)),
        "row", 0, 0, tiled=True, axis_index_groups=x_groups(),
    )
    a_mine = jnp.stack([a_two] + [lax.ppermute(a_two, "col", y_shift(s)) for s in (1, 2, 3)])
    a_other = lax.ppermute(a_mine, "col", core_swap())
    paired, send0, send1 = pair(place, a_mine, a_other, w_all)
    get0 = lax.ppermute(send0, ("row", "col"), mirror_perm(0))
    get1 = lax.ppermute(send1, ("row", "col"), mirror_perm(1))
    irrep_a = lax.dynamic_slice_in_dim(virtual_irrep, r * WA, WA)
    irrep_b = lax.dynamic_slice_in_dim(virtual_irrep, c * WB, WB)
    row_key = (occupied_irrep[:, None] ^ irrep_a[None, :]).reshape(SIDE, 1)
    row_key = jnp.broadcast_to(row_key, (SIDE, 128))
    col_key = (occupied_irrep[None, :, None] ^ irrep_b.reshape(2, 1, HALF)).reshape(2, SIDE)
    source = jnp.arange(SIDE)
    order = ((source % HALF) * OCC + source // HALF)[:, None] == jnp.arange(SIDE)[None, :]
    result = finish(place, paired, get0, get1, row_key, col_key, order.astype(jnp.bfloat16))
    return result.reshape(OCC, WA, WB * OCC)


def solution(mesh):
    return jax.shard_map(
        on_device,
        mesh=mesh,
        in_specs=(P(None, "row", "col"), P(None, "row", "col"), P(), P()),
        out_specs=P(None, "row", "col"),
        check_vma=False,
    )
```

```python
import jax
import jax.numpy as jnp
from jax import lax
from jax.experimental import pallas as pl
from jax.experimental.pallas import tpu as pltpu
from jax.sharding import PartitionSpec as P

Q, S, X = 2, 4, 4
H, Y, CORE = 2, 4, 2
ROWS, COLS = Q * S * X, H * Y * CORE
OCC, WA, WB = 12, 32, 64
HALF = 32
GROUPS = OCC // 4
SIDE = OCC * 32
TILES = 17
STEPS = (0, 1, 3, 2)
VMEM = pl.BlockSpec(memory_space=pltpu.VMEM)
SMEM = pl.BlockSpec(memory_space=pltpu.SMEM)
HBM = pl.BlockSpec(memory_space=pltpu.HBM)
PARAMS = pltpu.CompilerParams(vmem_limit_bytes=48 * 1024 * 1024)


def bf16(*shape):
    return jax.ShapeDtypeStruct(shape, jnp.bfloat16)


def s_shift(step):
    return [(r, r // 16 * 16 + (r // X % S + step) % S * X + r % X) for r in range(ROWS)]


def q_swap():
    return [(r, r ^ (S * X)) for r in range(ROWS)]


def x_groups():
    return [[z * X + x for x in range(X)] for z in range(Q * S)]


def h_swap():
    return [(c, c ^ (Y * CORE)) for c in range(COLS)]


def y_swap(step):
    return [(c, c ^ (2 if step == 1 else 6)) for c in range(COLS)]


def core_swap():
    return [(c, c ^ 1) for c in range(COLS)]


def mirror_perm(step):
    return [
        (r * COLS + c, (2 * c + (step + r) % 2) * COLS + r // 2)
        for r in range(ROWS) for c in range(COLS)
    ]


def slot_of(shape):
    return lax.broadcasted_iota(jnp.int32, shape, 1) // HALF


def crossed(load, i, group):
    slot = slot_of((32, 128))
    out = None
    for s in range(4):
        piece = load(4 * group + s, i // 4)
        shift = (s - i % 4) % 4
        if shift:
            piece = pltpu.roll(piece, shift * HALF, 1)
        out = piece if out is None else jnp.where(slot == s, piece, out)
    return out


def full_tiles():
    return [(i, g) for i in range(OCC) for g in range(i // 4 + 1, GROUPS)]


def pack_kernel(a_hbm, w_hbm, a_out, w_out, a_ref, w_ref, sem):
    copies = [pltpu.make_async_copy(w_hbm, w_ref, sem.at[0]), pltpu.make_async_copy(a_hbm, a_ref, sem.at[1])]
    for copy in copies:
        copy.start()
    for copy in copies:
        copy.wait()
    for i in range(OCC // 2):
        a_out[32 * i : 32 * i + 32, :] = jnp.concatenate([a_ref[i], a_ref[i + 6]], axis=1)
    for g in range(GROUPS):
        block = [w_ref[4 * g + s].astype(jnp.float32) for s in range(4)]
        for half in range(2):
            cut = jnp.concatenate([b[:, HALF * half : HALF * half + HALF] for b in block], axis=1)
            lane = half * SIDE + 128 * g
            w_out[:, lane : lane + 128] = cut.astype(jnp.bfloat16)


def pack(amplitudes, cycle_vertex):
    return pl.pallas_call(
        pack_kernel,
        out_shape=(bf16(192, 128), bf16(32, 2 * SIDE)),
        in_specs=[HBM, HBM],
        out_specs=(VMEM, VMEM),
        scratch_shapes=[
            pltpu.VMEM(amplitudes.shape, jnp.bfloat16),
            pltpu.VMEM(cycle_vertex.shape, jnp.bfloat16),
            pltpu.SemaphoreType.DMA((2,)),
        ],
        compiler_params=PARAMS,
        name="pack",
    )(amplitudes, cycle_vertex)


def keys_kernel(place_ref, occ_ref, virt_ref, row_key, col_key, order):
    r, c = place_ref[5], place_ref[6]

    def cut(first):
        line = jnp.broadcast_to(virt_ref[pl.ds(first // 128, 1), :], (8, 128))
        return pltpu.roll(line, lax.rem(128 - lax.rem(first, 128), 128), 1)

    down = jnp.broadcast_to(cut(WA * r)[:1], (128, 128)).T[:32]
    for i in range(OCC):
        row_key[32 * i : 32 * i + 32, :] = down ^ occ_ref[i]
    slot = slot_of((8, 128))
    for half in range(2):
        line = cut(WB * c + HALF * half)
        wide = line
        for s in range(1, 4):
            wide = jnp.where(slot == s, pltpu.roll(line, s * HALF, 1), wide)
        for g in range(GROUPS):
            label = jnp.full((8, 128), occ_ref[4 * g], jnp.int32)
            for s in range(1, 4):
                label = jnp.where(slot == s, occ_ref[4 * g + s], label)
            col_key[half : half + 1, 128 * g : 128 * g + 128] = (wide ^ label)[:1]
    source = lax.broadcasted_iota(jnp.int32, (SIDE, SIDE), 0)
    target = lax.broadcasted_iota(jnp.int32, (SIDE, SIDE), 1)
    hit = (source % HALF) * OCC + source // HALF == target
    order[...] = jnp.where(hit, 1.0, 0.0).astype(jnp.bfloat16)


def keys(place, occupied_irrep, virtual_irrep):
    return pl.pallas_call(
        keys_kernel,
        out_shape=(
            jax.ShapeDtypeStruct((SIDE, 128), jnp.int32),
            jax.ShapeDtypeStruct((2, SIDE), jnp.int32),
            bf16(SIDE, SIDE),
        ),
        in_specs=[SMEM, SMEM, VMEM],
        out_specs=(VMEM, VMEM, VMEM),
        compiler_params=PARAMS,
        name="keys",
    )(place, occupied_irrep, virtual_irrep.reshape(8, 128))


def paired_half(half, lhs, w_ref, paired_ref, send_ref, prod, turned):
    lanes = pl.ds(pl.multiple_of(half * SIDE, 128), SIDE)
    prod[...] = jnp.dot(
        jnp.concatenate([lhs[p] for p in range(Q * S)], axis=1),
        jnp.concatenate([w_ref[x, k, q, :, lanes] for k in range(S) for q in range(Q) for x in range(X)], axis=0),
        preferred_element_type=jnp.float32,
    )

    def load(j, group):
        return prod[32 * j : 32 * j + 32, 128 * group : 128 * group + 128]

    for i in range(OCC):
        for g in range(GROUPS):
            paired_ref[32 * i : 32 * i + 32, 128 * g : 128 * g + 128] = (
                load(i, g) - crossed(load, i, g)
            ).astype(jnp.bfloat16)
    turned[...] = paired_ref[...].astype(jnp.float32).T

    def tile(i, group):
        return turned[32 * i : 32 * i + 32, 128 * group : 128 * group + 128]

    slot = slot_of((32, 128))
    out = [tile(i, g) for i, g in full_tiles()]
    for q in range(GROUPS):
        out.append(jnp.where(slot == 0, pltpu.roll(tile(4 * q + 2, q), HALF, 1), tile(4 * q, q)))
    out.append(jnp.where(slot < 2, pltpu.roll(tile(5, 1), 2 * HALF, 1), tile(1, 0)))
    out.append(tile(9, 2))
    for t, value in enumerate(out):
        send_ref[32 * t : 32 * t + 32, :] = value.astype(jnp.bfloat16)


def first_kernel(place_ref, own_ref, far_ref, w_ref, lhs, paired_ref, send_ref, prod, turned):
    core, y, q_own, s_own = place_ref[1], place_ref[2], place_ref[3], place_ref[4]
    for step in range(Y):
        shift = lax.rem(s_own + S - jnp.bitwise_xor(y, STEPS[step]), S)
        k = jnp.bitwise_xor(shift, shift // 2)
        for h in range(H):
            mine, other = own_ref[step, h], far_ref[step, h]
            first = jnp.where(core == 0, mine, other)
            second = jnp.where(core == 0, other, mine)
            at = Q * k + jnp.bitwise_xor(q_own, h)
            lhs[at, :192] = jnp.concatenate([first[:, :64], second[:, :64]], axis=1)
            lhs[at, 192:] = jnp.concatenate([first[:, 64:], second[:, 64:]], axis=1)
    paired_half(place_ref[0], lhs, w_ref, paired_ref, send_ref, prod, turned)


def second_kernel(place_ref, lhs, w_ref, paired_ref, send_ref, prod, turned):
    paired_half(1 - place_ref[0], lhs, w_ref, paired_ref, send_ref, prod, turned)


WORK = [pltpu.VMEM((SIDE, SIDE), jnp.float32), pltpu.VMEM((SIDE, SIDE), jnp.float32)]


def pair_first(place, a_mine, a_other, w_all):
    return pl.pallas_call(
        first_kernel,
        out_shape=(bf16(Q * S, SIDE, 128), bf16(SIDE, SIDE), bf16(TILES * 32, 128)),
        in_specs=[SMEM, VMEM, VMEM, VMEM],
        out_specs=(VMEM, VMEM, VMEM),
        scratch_shapes=WORK,
        compiler_params=PARAMS,
        name="pair_first",
    )(place, a_mine, a_other, w_all)


def pair_second(place, lhs, w_all):
    return pl.pallas_call(
        second_kernel,
        out_shape=(bf16(SIDE, SIDE), bf16(TILES * 32, 128)),
        in_specs=[SMEM, VMEM, VMEM],
        out_specs=(VMEM, VMEM),
        scratch_shapes=WORK,
        compiler_params=PARAMS,
        name="pair_second",
    )(place, lhs, w_all)


def residual_half(half, paired_ref, get_ref, row_key, col_key, order, upper, whole):
    slot = slot_of((32, 128))

    def got(t):
        return get_ref[32 * t : 32 * t + 32, :].astype(jnp.float32)

    def put(i, group, mirrored, floor):
        rows, lanes = slice(32 * i, 32 * i + 32), slice(128 * group, 128 * group + 128)
        diff = paired_ref[rows, lanes].astype(jnp.float32) + mirrored
        if floor >= 0:
            diff = jnp.where(slot > floor, diff, 0.0)
        upper[rows, lanes] = diff

    for t, (i, g) in enumerate(full_tiles()):
        put(i, g, got(t), -1)
    last = [got(15), got(16)]
    for q in range(GROUPS):
        piece = got(12 + q)
        put(4 * q, q, piece, 0)
        put(4 * q + 2, q, pltpu.roll(piece, 3 * HALF, 1), 2)
        put(4 * q + 1, q, (last[0], pltpu.roll(last[0], 2 * HALF, 1), last[1])[q], 1)
        upper[32 * (4 * q + 3) : 32 * (4 * q + 4), 128 * q : 128 * q + 128] = jnp.zeros((32, 128), jnp.float32)

    def load(j, group):
        return upper[32 * j : 32 * j + 32, 128 * group : 128 * group + 128]

    col = jnp.where(half == 0, col_key[0:1, :], col_key[1:2, :])
    for i in range(OCC):
        rows = slice(32 * i, 32 * i + 32)
        for g in range(GROUPS):
            lanes = slice(128 * g, 128 * g + 128)
            if g > i // 4:
                value = load(i, g)
            elif g < i // 4:
                value = -crossed(load, i, g)
            else:
                value = load(i, g) - crossed(load, i, g)
            allowed = row_key[rows, :] == col[:, lanes]
            whole[rows, lanes] = jnp.where(allowed, value, 0.0).astype(jnp.bfloat16)
    return jnp.dot(whole[...], order[...], preferred_element_type=jnp.float32).astype(jnp.bfloat16)


def finish_first_kernel(place_ref, paired_ref, get_ref, row_key, col_key, order, out_ref, upper, whole):
    out_ref[...] = residual_half(place_ref[0], paired_ref, get_ref, row_key, col_key, order, upper, whole)


def finish_second_kernel(place_ref, done_ref, paired_ref, get_ref, row_key, col_key, order, out_ref, upper, whole):
    half = place_ref[0]
    out_ref[:, pl.ds(pl.multiple_of(half * SIDE, 128), SIDE)] = done_ref[...]
    out_ref[:, pl.ds(pl.multiple_of((1 - half) * SIDE, 128), SIDE)] = residual_half(
        1 - half, paired_ref, get_ref, row_key, col_key, order, upper, whole
    )


def finish(kernel, width, name, place, *arrays):
    return pl.pallas_call(
        kernel,
        out_shape=bf16(SIDE, width),
        in_specs=[SMEM] + [VMEM] * len(arrays),
        out_specs=VMEM,
        scratch_shapes=[pltpu.VMEM((SIDE, SIDE), jnp.float32), pltpu.VMEM((SIDE, SIDE), jnp.bfloat16)],
        compiler_params=PARAMS,
        name=name,
    )(place, *arrays)


def on_device(amplitudes, cycle_vertex, occupied_irrep, virtual_irrep):
    r, c = lax.axis_index("row"), lax.axis_index("col")
    place = jnp.stack([r % 2, c % 2, c // 2 % Y, r // (S * X), r // X % S, r, c]).astype(jnp.int32)
    a_own, w_own = pack(amplitudes, cycle_vertex)
    a_far = lax.ppermute(a_own, "col", h_swap())
    w_far = lax.ppermute(w_own, "row", q_swap())
    low = c < Y * CORE
    a_two = jnp.stack([jnp.where(low, a_own, a_far), jnp.where(low, a_far, a_own)])
    w_two = jnp.stack([w_own, w_far])
    w_z = jnp.stack([w_two] + [lax.ppermute(w_two, "row", s_shift(k)) for k in STEPS[1:]])
    w_z, a_two = lax.optimization_barrier((w_z, a_two))
    w_all = lax.all_to_all(
        jnp.broadcast_to(w_z[None], (X, S, Q, 32, 2 * SIDE)), "row", 0, 0, tiled=True, axis_index_groups=x_groups()
    )
    a_pair = jnp.stack([a_two, lax.ppermute(a_two, "col", y_swap(1))])
    a_mine = jnp.concatenate([a_pair, lax.ppermute(a_pair, "col", y_swap(2))])
    a_other = lax.ppermute(a_mine, "col", core_swap())
    row_key, col_key, order = keys(place, occupied_irrep, virtual_irrep)
    lhs, paired0, send0 = pair_first(place, a_mine, a_other, w_all)
    get0 = lax.ppermute(send0, ("row", "col"), mirror_perm(0))
    paired1, send1 = pair_second(place, lhs, w_all)
    get1 = lax.ppermute(send1, ("row", "col"), mirror_perm(1))
    done = finish(finish_first_kernel, SIDE, "finish_first", place, paired0, get0, row_key, col_key, order)
    result = finish(
        finish_second_kernel, 2 * SIDE, "finish_second", place, done, paired1, get1, row_key, col_key, order
    )
    return result.reshape(OCC, WA, WB * OCC)


def solution(mesh):
    return jax.shard_map(
        on_device,
        mesh=mesh,
        in_specs=(P(None, "row", "col"), P(None, "row", "col"), P(), P()),
        out_specs=P(None, "row", "col"),
        check_vma=False,
    )
```

```python
import functools

import jax
import jax.numpy as jnp
from jax import lax
from jax.experimental import pallas as pl
from jax.experimental.pallas import tpu as pltpu
from jax.sharding import PartitionSpec as P

Q, S, X = 2, 4, 4
H, Y, CORE = 2, 4, 2
ROWS, COLS = Q * S * X, H * Y * CORE
OCC, WA, WB = 12, 32, 64
HALF = 32
GROUPS = OCC // 4
SIDE = OCC * 32
TILES = 17
STEPS = (0, 1, 3, 2)
PARTS = [slice(r, r + 96) for r in range(0, SIDE, 96)]
VMEM = pl.BlockSpec(memory_space=pltpu.VMEM)
SMEM = pl.BlockSpec(memory_space=pltpu.SMEM)
HBM = pl.BlockSpec(memory_space=pltpu.HBM)
PARAMS = pltpu.CompilerParams(vmem_limit_bytes=48 * 1024 * 1024)


def bf16(*shape):
    return jax.ShapeDtypeStruct(shape, jnp.bfloat16)


def s_shift(step):
    return [(r, r // 16 * 16 + (r // X % S + step) % S * X + r % X) for r in range(ROWS)]


def q_swap():
    return [(r, r ^ (S * X)) for r in range(ROWS)]


def x_groups():
    return [[z * X + x for x in range(X)] for z in range(Q * S)]


def h_swap():
    return [(c, c ^ (Y * CORE)) for c in range(COLS)]


def y_swap(step):
    return [(c, c ^ (CORE * step)) for c in range(COLS)]


def core_swap():
    return [(c, c ^ 1) for c in range(COLS)]


def mirror_perm(step):
    return [
        (r * COLS + c, (2 * c + (step + r) % 2) * COLS + r // 2)
        for r in range(ROWS) for c in range(COLS)
    ]


def slot_of(shape):
    return lax.broadcasted_iota(jnp.int32, shape, 1) // HALF


def crossed(load, i, group):
    slot = slot_of((32, 128))
    out = None
    for s in range(4):
        piece = load(4 * group + s, i // 4)
        shift = (s - i % 4) % 4
        if shift:
            piece = pltpu.roll(piece, shift * HALF, 1)
        out = piece if out is None else jnp.where(slot == s, piece, out)
    return out


def full_tiles():
    return [(i, g) for i in range(OCC) for g in range(i // 4 + 1, GROUPS)]


def pack_w_kernel(w_ref, w_out):
    for g in range(GROUPS):
        block = [w_ref[4 * g + s].astype(jnp.float32) for s in range(4)]
        for half in range(2):
            cut = jnp.concatenate([b[:, HALF * half : HALF * half + HALF] for b in block], axis=1)
            lane = half * SIDE + 128 * g
            w_out[:, lane : lane + 128] = cut.astype(jnp.bfloat16)


def pack_a_kernel(a_ref, a_out):
    for i in range(OCC // 2):
        a_out[32 * i : 32 * i + 32, :] = jnp.concatenate([a_ref[i], a_ref[i + 6]], axis=1)


def pack(kernel, shape, name, array):
    return pl.pallas_call(
        kernel,
        out_shape=bf16(*shape),
        in_specs=[VMEM],
        out_specs=VMEM,
        compiler_params=PARAMS,
        name=name,
    )(array)


def spread_kernel(first, count, *refs):
    blocks, out, sem = refs[-count - 2 : -2], refs[-2], refs[-1]
    copies = [
        pltpu.make_async_copy(blocks[k], out.at[x, first + k], sem.at[count * x + k])
        for x in range(X) for k in range(count)
    ]
    for copy in copies:
        copy.start()
    for copy in copies:
        copy.wait()


def spread(first, blocks, begun, name):
    count = len(blocks)
    return pl.pallas_call(
        functools.partial(spread_kernel, first, count),
        out_shape=bf16(X, S, *blocks[0].shape),
        in_specs=[HBM] * len(begun) + [VMEM] * count,
        out_specs=HBM,
        scratch_shapes=[pltpu.SemaphoreType.DMA((count * X,))],
        input_output_aliases={0: 0} if begun else {},
        compiler_params=PARAMS,
        name=name,
    )(*begun, *blocks)


def keys_kernel(place_ref, occ_ref, virt_ref, row_key, col_key, order):
    r, c = place_ref[5], place_ref[6]

    def cut(first):
        line = jnp.broadcast_to(virt_ref[pl.ds(first // 128, 1), :], (8, 128))
        return pltpu.roll(line, lax.rem(128 - lax.rem(first, 128), 128), 1)

    down = jnp.broadcast_to(cut(WA * r)[:1], (128, 128)).T[:32]
    for i in range(OCC):
        row_key[32 * i : 32 * i + 32, :] = down ^ occ_ref[i]
    slot = slot_of((8, 128))
    for half in range(2):
        line = cut(WB * c + HALF * half)
        wide = line
        for s in range(1, 4):
            wide = jnp.where(slot == s, pltpu.roll(line, s * HALF, 1), wide)
        for g in range(GROUPS):
            label = jnp.full((8, 128), occ_ref[4 * g], jnp.int32)
            for s in range(1, 4):
                label = jnp.where(slot == s, occ_ref[4 * g + s], label)
            col_key[half : half + 1, 128 * g : 128 * g + 128] = (wide ^ label)[:1]
    source = lax.broadcasted_iota(jnp.int32, (SIDE, SIDE), 0)
    target = lax.broadcasted_iota(jnp.int32, (SIDE, SIDE), 1)
    hit = (source % HALF) * OCC + source // HALF == target
    order[...] = jnp.where(hit, 1.0, 0.0).astype(jnp.bfloat16)


def keys(place, occupied_irrep, virtual_irrep):
    return pl.pallas_call(
        keys_kernel,
        out_shape=(
            jax.ShapeDtypeStruct((SIDE, 128), jnp.int32),
            jax.ShapeDtypeStruct((2, SIDE), jnp.int32),
            bf16(SIDE, SIDE),
        ),
        in_specs=[SMEM, SMEM, VMEM],
        out_specs=(VMEM, VMEM, VMEM),
        compiler_params=PARAMS,
        name="keys",
    )(place, occupied_irrep, virtual_irrep.reshape(8, 128))


def paired_half(half, lhs, w_ref, paired_ref, send_ref, prod, turned):
    lanes = pl.ds(pl.multiple_of(half * SIDE, 128), SIDE)
    prod[...] = jnp.dot(
        jnp.concatenate([lhs[p] for p in range(Q * S)], axis=1),
        jnp.concatenate([w_ref[x, k, q, :, lanes] for k in range(S) for q in range(Q) for x in range(X)], axis=0),
        preferred_element_type=jnp.float32,
    )

    def load(j, group):
        return prod[32 * j : 32 * j + 32, 128 * group : 128 * group + 128]

    for i in range(OCC):
        for g in range(GROUPS):
            paired_ref[32 * i : 32 * i + 32, 128 * g : 128 * g + 128] = (
                load(i, g) - crossed(load, i, g)
            ).astype(jnp.bfloat16)
    turned[...] = paired_ref[...].astype(jnp.float32).T

    def tile(i, group):
        return turned[32 * i : 32 * i + 32, 128 * group : 128 * group + 128]

    slot = slot_of((32, 128))
    out = [tile(i, g) for i, g in full_tiles()]
    for q in range(GROUPS):
        out.append(jnp.where(slot == 0, pltpu.roll(tile(4 * q + 2, q), HALF, 1), tile(4 * q, q)))
    out.append(jnp.where(slot < 2, pltpu.roll(tile(5, 1), 2 * HALF, 1), tile(1, 0)))
    out.append(tile(9, 2))
    for t, value in enumerate(out):
        send_ref[32 * t : 32 * t + 32, :] = value.astype(jnp.bfloat16)


def first_kernel(place_ref, own_ref, far_ref, w_ref, lhs, paired_ref, send_ref, prod, turned):
    core, y, q_own, s_own = place_ref[1], place_ref[2], place_ref[3], place_ref[4]
    for step in range(Y):
        shift = lax.rem(s_own + S - jnp.bitwise_xor(y, STEPS[step]), S)
        k = jnp.bitwise_xor(shift, shift // 2)
        for h in range(H):
            mine, other = own_ref[step, h], far_ref[step, h]
            first = jnp.where(core == 0, mine, other)
            second = jnp.where(core == 0, other, mine)
            at = Q * k + jnp.bitwise_xor(q_own, h)
            lhs[at, :192] = jnp.concatenate([first[:, :64], second[:, :64]], axis=1)
            lhs[at, 192:] = jnp.concatenate([first[:, 64:], second[:, 64:]], axis=1)
    paired_half(place_ref[0], lhs, w_ref, paired_ref, send_ref, prod, turned)


def second_kernel(place_ref, lhs, w_ref, paired_ref, send_ref, prod, turned):
    paired_half(1 - place_ref[0], lhs, w_ref, paired_ref, send_ref, prod, turned)


WORK = [pltpu.VMEM((SIDE, SIDE), jnp.float32), pltpu.VMEM((SIDE, SIDE), jnp.float32)]


def pair_first(place, a_mine, a_other, w_all):
    return pl.pallas_call(
        first_kernel,
        out_shape=(bf16(Q * S, SIDE, 128), bf16(SIDE, SIDE), bf16(TILES * 32, 128)),
        in_specs=[SMEM, VMEM, VMEM, VMEM],
        out_specs=(VMEM, VMEM, VMEM),
        scratch_shapes=WORK,
        compiler_params=PARAMS,
        name="pair_first",
    )(place, a_mine, a_other, w_all)


def pair_second(place, lhs, w_all):
    return pl.pallas_call(
        second_kernel,
        out_shape=(bf16(SIDE, SIDE), bf16(TILES * 32, 128)),
        in_specs=[SMEM, VMEM, VMEM],
        out_specs=(VMEM, VMEM),
        scratch_shapes=WORK,
        compiler_params=PARAMS,
        name="pair_second",
    )(place, lhs, w_all)


def residual_half(half, paired_ref, get_ref, row_key, col_key, order, upper, whole):
    slot = slot_of((32, 128))

    def got(t):
        return get_ref[32 * t : 32 * t + 32, :].astype(jnp.float32)

    def put(i, group, mirrored, floor):
        rows, lanes = slice(32 * i, 32 * i + 32), slice(128 * group, 128 * group + 128)
        diff = paired_ref[rows, lanes].astype(jnp.float32) + mirrored
        if floor >= 0:
            diff = jnp.where(slot > floor, diff, 0.0)
        upper[rows, lanes] = diff

    for t, (i, g) in enumerate(full_tiles()):
        put(i, g, got(t), -1)
    last = [got(15), got(16)]
    for q in range(GROUPS):
        piece = got(12 + q)
        put(4 * q, q, piece, 0)
        put(4 * q + 2, q, pltpu.roll(piece, 3 * HALF, 1), 2)
        put(4 * q + 1, q, (last[0], pltpu.roll(last[0], 2 * HALF, 1), last[1])[q], 1)
        upper[32 * (4 * q + 3) : 32 * (4 * q + 4), 128 * q : 128 * q + 128] = jnp.zeros((32, 128), jnp.float32)

    def load(j, group):
        return upper[32 * j : 32 * j + 32, 128 * group : 128 * group + 128]

    col = jnp.where(half == 0, col_key[0:1, :], col_key[1:2, :])
    for i in range(OCC):
        rows = slice(32 * i, 32 * i + 32)
        for g in range(GROUPS):
            lanes = slice(128 * g, 128 * g + 128)
            if g > i // 4:
                value = load(i, g)
            elif g < i // 4:
                value = -crossed(load, i, g)
            else:
                value = load(i, g) - crossed(load, i, g)
            allowed = row_key[rows, :] == col[:, lanes]
            whole[rows, lanes] = jnp.where(allowed, value, 0.0).astype(jnp.bfloat16)
    for rows in PARTS:
        yield rows, jnp.dot(whole[rows, :], order[...], preferred_element_type=jnp.float32).astype(jnp.bfloat16)


def half_lanes(half):
    return pl.ds(pl.multiple_of(half * SIDE, 128), SIDE)


def finish_first_kernel(place_ref, paired_ref, get_ref, row_key, col_key, order, done_ref, upper, whole):
    for rows, value in residual_half(place_ref[0], paired_ref, get_ref, row_key, col_key, order, upper, whole):
        done_ref[rows, :] = value


def finish_second_kernel(
    place_ref, done_ref, paired_ref, get_ref, row_key, col_key, order, out_ref, upper, whole, result, sem
):
    half = place_ref[0]
    copies = [pltpu.make_async_copy(done_ref, out_ref.at[:, half_lanes(half)], sem.at[len(PARTS)])]
    copies[0].start()
    for rows, value in residual_half(1 - half, paired_ref, get_ref, row_key, col_key, order, upper, whole):
        result[rows, :] = value
        copies.append(
            pltpu.make_async_copy(result.at[rows], out_ref.at[rows, half_lanes(1 - half)], sem.at[len(copies) - 1])
        )
        copies[-1].start()
    for copy in copies:
        copy.wait()


def finish(kernel, width, out_space, scratch, name, place, *arrays):
    return pl.pallas_call(
        kernel,
        out_shape=bf16(SIDE, width),
        in_specs=[SMEM] + [VMEM] * len(arrays),
        out_specs=out_space,
        scratch_shapes=[pltpu.VMEM((SIDE, SIDE), jnp.float32), pltpu.VMEM((SIDE, SIDE), jnp.bfloat16)] + scratch,
        compiler_params=PARAMS,
        name=name,
    )(place, *arrays)


def on_device(amplitudes, cycle_vertex, occupied_irrep, virtual_irrep):
    r, c = lax.axis_index("row"), lax.axis_index("col")
    place = jnp.stack([r % 2, c % 2, c // 2 % Y, r // (S * X), r // X % S, r, c]).astype(jnp.int32)
    w_own = pack(pack_w_kernel, (32, 2 * SIDE), "pack_w", cycle_vertex)
    a_own = pack(pack_a_kernel, (192, 128), "pack_a", amplitudes)
    a_far = lax.ppermute(a_own, "col", h_swap())
    w_far = lax.ppermute(w_own, "row", q_swap())
    low = c < Y * CORE
    a_two = jnp.stack([jnp.where(low, a_own, a_far), jnp.where(low, a_far, a_own)])
    w_two = jnp.stack([w_own, w_far])
    w_s = [lax.ppermute(w_two, "row", s_shift(k)) for k in STEPS[1:]]
    w_s[0], a_two = lax.optimization_barrier((w_s[0], a_two))
    a_next = lax.ppermute(a_two, "col", y_swap(1))
    w_wide = spread(0, [w_two] + w_s[:2], (), "spread_first")
    w_s, w_wide, a_two, a_next = lax.optimization_barrier((w_s, w_wide, a_two, a_next))
    w_wide = spread(S - 1, w_s[2:], (w_wide,), "spread_last")
    w_all = lax.all_to_all(w_wide, "row", 0, 0, tiled=True, axis_index_groups=x_groups())
    a_mine = jnp.stack([a_two, a_next] + [lax.ppermute(a_two, "col", y_swap(k)) for k in STEPS[2:]])
    a_other = lax.ppermute(a_mine, "col", core_swap())
    row_key, col_key, order = keys(place, occupied_irrep, virtual_irrep)
    lhs, paired0, send0 = pair_first(place, a_mine, a_other, w_all)
    get0 = lax.ppermute(send0, ("row", "col"), mirror_perm(0))
    paired1, send1 = pair_second(place, lhs, w_all)
    get1 = lax.ppermute(send1, ("row", "col"), mirror_perm(1))
    keep = (row_key, col_key, order)
    done = finish(finish_first_kernel, SIDE, VMEM, [], "finish_first", place, paired0, get0, *keep)
    last = [pltpu.VMEM((SIDE, SIDE), jnp.bfloat16), pltpu.SemaphoreType.DMA((len(PARTS) + 1,))]
    result = finish(
        finish_second_kernel, 2 * SIDE, HBM, last, "finish_second", place, done, paired1, get1, *keep
    )
    return result.reshape(OCC, WA, WB * OCC)


def solution(mesh):
    return jax.shard_map(
        on_device,
        mesh=mesh,
        in_specs=(P(None, "row", "col"), P(None, "row", "col"), P(), P()),
        out_specs=P(None, "row", "col"),
        check_vma=False,
    )
```

```python
import functools

import jax
import jax.numpy as jnp
from jax import lax
from jax.experimental import pallas as pl
from jax.experimental.pallas import tpu as pltpu
from jax.sharding import PartitionSpec as P

Q, S, X = 2, 4, 4
H, Y, CORE = 2, 4, 2
ROWS, COLS = Q * S * X, H * Y * CORE
OCC, WA, WB = 12, 32, 64
HALF = 32
GROUPS = OCC // 4
SIDE = OCC * 32
SENT = 16 * 32 + 16
STEPS = (0, 1, 3, 2)
PARTS = [slice(r, r + 96) for r in range(0, SIDE, 96)]
VMEM = pl.BlockSpec(memory_space=pltpu.VMEM)
SMEM = pl.BlockSpec(memory_space=pltpu.SMEM)
HBM = pl.BlockSpec(memory_space=pltpu.HBM)
PARAMS = pltpu.CompilerParams(vmem_limit_bytes=48 * 1024 * 1024)


def bf16(*shape):
    return jax.ShapeDtypeStruct(shape, jnp.bfloat16)


def s_shift(step):
    return [(r, r // 16 * 16 + (r // X % S + step) % S * X + r % X) for r in range(ROWS)]


def q_swap():
    return [(r, r ^ (S * X)) for r in range(ROWS)]


def x_groups():
    return [[z * X + x for x in range(X)] for z in range(Q * S)]


def h_swap():
    return [(c, c ^ (Y * CORE)) for c in range(COLS)]


def y_swap(step):
    return [(c, c ^ (CORE * step)) for c in range(COLS)]


def core_swap():
    return [(c, c ^ 1) for c in range(COLS)]


def mirror_perm(step):
    return [
        (r * COLS + c, (2 * c + (step + r) % 2) * COLS + r // 2)
        for r in range(ROWS) for c in range(COLS)
    ]


def slot_of(shape):
    return lax.broadcasted_iota(jnp.int32, shape, 1) // HALF


def crossed(load, i, group):
    slot = slot_of((32, 128))
    out = None
    for s in range(4):
        piece = load(4 * group + s, i // 4)
        shift = (s - i % 4) % 4
        if shift:
            piece = pltpu.roll(piece, shift * HALF, 1)
        out = piece if out is None else jnp.where(slot == s, piece, out)
    return out


def full_tiles():
    return [(i, g) for i in range(OCC) for g in range(i // 4 + 1, GROUPS)]


def pack_w_kernel(w_ref, w_out):
    for g in range(GROUPS):
        block = [w_ref[4 * g + s].astype(jnp.float32) for s in range(4)]
        for half in range(2):
            cut = jnp.concatenate([b[:, HALF * half : HALF * half + HALF] for b in block], axis=1)
            lane = half * SIDE + 128 * g
            w_out[:, lane : lane + 128] = cut.astype(jnp.bfloat16)


def pack_a_kernel(a_ref, a_out):
    for i in range(OCC // 2):
        a_out[32 * i : 32 * i + 32, :] = jnp.concatenate([a_ref[i], a_ref[i + 6]], axis=1)


def pack(kernel, shape, name, array):
    return pl.pallas_call(
        kernel,
        out_shape=bf16(*shape),
        in_specs=[VMEM],
        out_specs=VMEM,
        compiler_params=PARAMS,
        name=name,
    )(array)


def spread_kernel(first, count, *refs):
    blocks, out, sem = refs[-count - 2 : -2], refs[-2], refs[-1]
    copies = [
        pltpu.make_async_copy(blocks[k], out.at[x, first + k], sem.at[count * x + k])
        for x in range(X) for k in range(count)
    ]
    for copy in copies:
        copy.start()
    for copy in copies:
        copy.wait()


def spread(first, blocks, begun, name):
    count = len(blocks)
    return pl.pallas_call(
        functools.partial(spread_kernel, first, count),
        out_shape=bf16(X, S, *blocks[0].shape),
        in_specs=[HBM] * len(begun) + [VMEM] * count,
        out_specs=HBM,
        scratch_shapes=[pltpu.SemaphoreType.DMA((count * X,))],
        input_output_aliases={0: 0} if begun else {},
        compiler_params=PARAMS,
        name=name,
    )(*begun, *blocks)


def keys_kernel(place_ref, occ_ref, virt_ref, row_key, col_key, order):
    r, c = place_ref[5], place_ref[6]

    def cut(first):
        line = jnp.broadcast_to(virt_ref[pl.ds(first // 128, 1), :], (8, 128))
        return pltpu.roll(line, lax.rem(128 - lax.rem(first, 128), 128), 1)

    down = jnp.broadcast_to(cut(WA * r)[:1], (128, 128)).T[:32]
    for i in range(OCC):
        row_key[32 * i : 32 * i + 32, :] = down ^ occ_ref[i]
    slot = slot_of((8, 128))
    for half in range(2):
        line = cut(WB * c + HALF * half)
        wide = line
        for s in range(1, 4):
            wide = jnp.where(slot == s, pltpu.roll(line, s * HALF, 1), wide)
        for g in range(GROUPS):
            label = jnp.full((8, 128), occ_ref[4 * g], jnp.int32)
            for s in range(1, 4):
                label = jnp.where(slot == s, occ_ref[4 * g + s], label)
            col_key[half : half + 1, 128 * g : 128 * g + 128] = (wide ^ label)[:1]
    source = lax.broadcasted_iota(jnp.int32, (SIDE, SIDE), 0)
    target = lax.broadcasted_iota(jnp.int32, (SIDE, SIDE), 1)
    hit = (source % HALF) * OCC + source // HALF == target
    order[...] = jnp.where(hit, 1.0, 0.0).astype(jnp.bfloat16)


def keys(place, occupied_irrep, virtual_irrep):
    return pl.pallas_call(
        keys_kernel,
        out_shape=(
            jax.ShapeDtypeStruct((SIDE, 128), jnp.int32),
            jax.ShapeDtypeStruct((2, SIDE), jnp.int32),
            bf16(SIDE, SIDE),
        ),
        in_specs=[SMEM, SMEM, VMEM],
        out_specs=(VMEM, VMEM, VMEM),
        compiler_params=PARAMS,
        name="keys",
    )(place, occupied_irrep, virtual_irrep.reshape(8, 128))


def paired_half(half, lhs, w_ref, paired_ref, send_ref, prod, turned):
    lanes = pl.ds(pl.multiple_of(half * SIDE, 128), SIDE)
    prod[...] = jnp.dot(
        jnp.concatenate([lhs[p] for p in range(Q * S)], axis=1),
        jnp.concatenate([w_ref[x, k, q, :, lanes] for k in range(S) for q in range(Q) for x in range(X)], axis=0),
        preferred_element_type=jnp.float32,
    )

    def load(j, group):
        return prod[32 * j : 32 * j + 32, 128 * group : 128 * group + 128]

    for i in range(OCC):
        for g in range(GROUPS):
            paired_ref[32 * i : 32 * i + 32, 128 * g : 128 * g + 128] = (
                load(i, g) - crossed(load, i, g)
            ).astype(jnp.bfloat16)
    turned[...] = paired_ref[...].astype(jnp.float32).T

    def tile(i, group):
        return turned[32 * i : 32 * i + 32, 128 * group : 128 * group + 128]

    slot = slot_of((32, 128))
    out = [tile(i, g) for i, g in full_tiles()]
    for q in range(GROUPS):
        out.append(jnp.where(slot == 0, pltpu.roll(tile(4 * q + 2, q), HALF, 1), tile(4 * q, q)))
    out.append(jnp.where(slot < 2, pltpu.roll(tile(5, 1), 2 * HALF, 1), tile(1, 0)))
    for t, value in enumerate(out):
        send_ref[32 * t : 32 * t + 32, :] = value.astype(jnp.bfloat16)
    rest = tile(9, 2)
    rest = jnp.where(slot[:16] < 2, pltpu.roll(rest[16:], 2 * HALF, 1), rest[:16])
    send_ref[SENT - 16 :, :] = rest.astype(jnp.bfloat16)


def first_kernel(place_ref, own_ref, far_ref, w_ref, lhs, paired_ref, send_ref, prod, turned):
    core, y, q_own, s_own = place_ref[1], place_ref[2], place_ref[3], place_ref[4]
    for step in range(Y):
        shift = lax.rem(s_own + S - jnp.bitwise_xor(y, STEPS[step]), S)
        k = jnp.bitwise_xor(shift, shift // 2)
        for h in range(H):
            mine, other = own_ref[step, h], far_ref[step, h]
            first = jnp.where(core == 0, mine, other)
            second = jnp.where(core == 0, other, mine)
            at = Q * k + jnp.bitwise_xor(q_own, h)
            lhs[at, :192] = jnp.concatenate([first[:, :64], second[:, :64]], axis=1)
            lhs[at, 192:] = jnp.concatenate([first[:, 64:], second[:, 64:]], axis=1)
    paired_half(place_ref[0], lhs, w_ref, paired_ref, send_ref, prod, turned)


def second_kernel(place_ref, lhs, w_ref, paired_ref, send_ref, prod, turned):
    paired_half(1 - place_ref[0], lhs, w_ref, paired_ref, send_ref, prod, turned)


WORK = [pltpu.VMEM((SIDE, SIDE), jnp.float32), pltpu.VMEM((SIDE, SIDE), jnp.float32)]


def pair_first(place, a_mine, a_other, w_all):
    return pl.pallas_call(
        first_kernel,
        out_shape=(bf16(Q * S, SIDE, 128), bf16(SIDE, SIDE), bf16(SENT, 128)),
        in_specs=[SMEM, VMEM, VMEM, VMEM],
        out_specs=(VMEM, VMEM, VMEM),
        scratch_shapes=WORK,
        compiler_params=PARAMS,
        name="pair_first",
    )(place, a_mine, a_other, w_all)


def pair_second(place, lhs, w_all):
    return pl.pallas_call(
        second_kernel,
        out_shape=(bf16(SIDE, SIDE), bf16(SENT, 128)),
        in_specs=[SMEM, VMEM, VMEM],
        out_specs=(VMEM, VMEM),
        scratch_shapes=WORK,
        compiler_params=PARAMS,
        name="pair_second",
    )(place, lhs, w_all)


def residual_half(half, paired_ref, get_ref, row_key, col_key, order, upper, whole):
    slot = slot_of((32, 128))

    def got(t):
        return get_ref[32 * t : 32 * t + 32, :].astype(jnp.float32)

    def put(i, group, mirrored, floor):
        rows, lanes = slice(32 * i, 32 * i + 32), slice(128 * group, 128 * group + 128)
        diff = paired_ref[rows, lanes].astype(jnp.float32) + mirrored
        if floor >= 0:
            diff = jnp.where(slot > floor, diff, 0.0)
        upper[rows, lanes] = diff

    for t, (i, g) in enumerate(full_tiles()):
        put(i, g, got(t), -1)
    rest = get_ref[SENT - 16 :, :].astype(jnp.float32)
    last = [got(15), jnp.concatenate([rest, pltpu.roll(rest, 2 * HALF, 1)], axis=0)]
    for q in range(GROUPS):
        piece = got(12 + q)
        put(4 * q, q, piece, 0)
        put(4 * q + 2, q, pltpu.roll(piece, 3 * HALF, 1), 2)
        put(4 * q + 1, q, (last[0], pltpu.roll(last[0], 2 * HALF, 1), last[1])[q], 1)
        upper[32 * (4 * q + 3) : 32 * (4 * q + 4), 128 * q : 128 * q + 128] = jnp.zeros((32, 128), jnp.float32)

    def load(j, group):
        return upper[32 * j : 32 * j + 32, 128 * group : 128 * group + 128]

    col = jnp.where(half == 0, col_key[0:1, :], col_key[1:2, :])
    for i in range(OCC):
        rows = slice(32 * i, 32 * i + 32)
        for g in range(GROUPS):
            lanes = slice(128 * g, 128 * g + 128)
            if g > i // 4:
                value = load(i, g)
            elif g < i // 4:
                value = -crossed(load, i, g)
            else:
                value = load(i, g) - crossed(load, i, g)
            allowed = row_key[rows, :] == col[:, lanes]
            whole[rows, lanes] = jnp.where(allowed, value, 0.0).astype(jnp.bfloat16)
    for rows in PARTS:
        yield rows, jnp.dot(whole[rows, :], order[...], preferred_element_type=jnp.float32).astype(jnp.bfloat16)


def half_lanes(half):
    return pl.ds(pl.multiple_of(half * SIDE, 128), SIDE)


def finish_first_kernel(place_ref, paired_ref, get_ref, row_key, col_key, order, done_ref, upper, whole):
    for rows, value in residual_half(place_ref[0], paired_ref, get_ref, row_key, col_key, order, upper, whole):
        done_ref[rows, :] = value


def finish_second_kernel(
    place_ref, done_ref, paired_ref, get_ref, row_key, col_key, order, out_ref, upper, whole, result, sem
):
    half = place_ref[0]
    copies = [pltpu.make_async_copy(done_ref, out_ref.at[:, half_lanes(half)], sem.at[len(PARTS)])]
    copies[0].start()
    for rows, value in residual_half(1 - half, paired_ref, get_ref, row_key, col_key, order, upper, whole):
        result[rows, :] = value
        copies.append(
            pltpu.make_async_copy(result.at[rows], out_ref.at[rows, half_lanes(1 - half)], sem.at[len(copies) - 1])
        )
        copies[-1].start()
    for copy in copies:
        copy.wait()


def finish(kernel, width, out_space, scratch, name, place, *arrays):
    return pl.pallas_call(
        kernel,
        out_shape=bf16(SIDE, width),
        in_specs=[SMEM] + [VMEM] * len(arrays),
        out_specs=out_space,
        scratch_shapes=[pltpu.VMEM((SIDE, SIDE), jnp.float32), pltpu.VMEM((SIDE, SIDE), jnp.bfloat16)] + scratch,
        compiler_params=PARAMS,
        name=name,
    )(place, *arrays)


def on_device(amplitudes, cycle_vertex, occupied_irrep, virtual_irrep):
    r, c = lax.axis_index("row"), lax.axis_index("col")
    place = jnp.stack([r % 2, c % 2, c // 2 % Y, r // (S * X), r // X % S, r, c]).astype(jnp.int32)
    w_own = pack(pack_w_kernel, (32, 2 * SIDE), "pack_w", cycle_vertex)
    a_own = pack(pack_a_kernel, (192, 128), "pack_a", amplitudes)
    a_far = lax.ppermute(a_own, "col", h_swap())
    w_far = lax.ppermute(w_own, "row", q_swap())
    low = c < Y * CORE
    a_two = jnp.stack([jnp.where(low, a_own, a_far), jnp.where(low, a_far, a_own)])
    w_two = jnp.stack([w_own, w_far])
    w_s = [lax.ppermute(w_two, "row", s_shift(k)) for k in STEPS[1:]]
    w_s[0], a_two = lax.optimization_barrier((w_s[0], a_two))
    a_next = lax.ppermute(a_two, "col", y_swap(1))
    w_wide = spread(0, [w_two] + w_s[:2], (), "spread_first")
    w_s, w_wide, a_two, a_next = lax.optimization_barrier((w_s, w_wide, a_two, a_next))
    w_wide = spread(S - 1, w_s[2:], (w_wide,), "spread_last")
    w_all = lax.all_to_all(w_wide, "row", 0, 0, tiled=True, axis_index_groups=x_groups())
    a_mine = jnp.stack([a_two, a_next] + [lax.ppermute(a_two, "col", y_swap(k)) for k in STEPS[2:]])
    a_other = lax.ppermute(a_mine, "col", core_swap())
    row_key, col_key, order = keys(place, occupied_irrep, virtual_irrep)
    lhs, paired0, send0 = pair_first(place, a_mine, a_other, w_all)
    get0 = lax.ppermute(send0, ("row", "col"), mirror_perm(0))
    paired1, send1 = pair_second(place, lhs, w_all)
    get1 = lax.ppermute(send1, ("row", "col"), mirror_perm(1))
    keep = (row_key, col_key, order)
    done = finish(finish_first_kernel, SIDE, VMEM, [], "finish_first", place, paired0, get0, *keep)
    last = [pltpu.VMEM((SIDE, SIDE), jnp.bfloat16), pltpu.SemaphoreType.DMA((len(PARTS) + 1,))]
    result = finish(
        finish_second_kernel, 2 * SIDE, HBM, last, "finish_second", place, done, paired1, get1, *keep
    )
    return result.reshape(OCC, WA, WB * OCC)


def solution(mesh):
    return jax.shard_map(
        on_device,
        mesh=mesh,
        in_specs=(P(None, "row", "col"), P(None, "row", "col"), P(), P()),
        out_specs=P(None, "row", "col"),
        check_vma=False,
    )
```

```python
import functools

import jax
import jax.numpy as jnp
from jax import lax
from jax.experimental import pallas as pl
from jax.experimental.pallas import tpu as pltpu
from jax.sharding import PartitionSpec as P

Q, S, X = 2, 4, 4
H, Y, CORE = 2, 4, 2
ROWS, COLS = Q * S * X, H * Y * CORE
OCC, WA, WB = 12, 32, 64
HALF = 32
GROUPS = OCC // 4
SIDE = OCC * 32
SENT = 16 * 32 + 16
STEPS = (0, 1, 3, 2)
PARTS = [slice(r, r + 96) for r in range(0, SIDE, 96)]
VMEM = pl.BlockSpec(memory_space=pltpu.VMEM)
SMEM = pl.BlockSpec(memory_space=pltpu.SMEM)
HBM = pl.BlockSpec(memory_space=pltpu.HBM)
PARAMS = pltpu.CompilerParams(vmem_limit_bytes=48 * 1024 * 1024)


def bf16(*shape):
    return jax.ShapeDtypeStruct(shape, jnp.bfloat16)


def s_shift(step):
    return [(r, r // 16 * 16 + (r // X % S + step) % S * X + r % X) for r in range(ROWS)]


def q_swap():
    return [(r, r ^ (S * X)) for r in range(ROWS)]


def x_groups():
    return [[z * X + x for x in range(X)] for z in range(Q * S)]


def h_swap():
    return [(c, c ^ (Y * CORE)) for c in range(COLS)]


def y_swap(step):
    return [(c, c ^ (CORE * step)) for c in range(COLS)]


def core_swap():
    return [(c, c ^ 1) for c in range(COLS)]


def mirror_perm(step):
    return [
        (r * COLS + c, (2 * c + (step + r) % 2) * COLS + r // 2)
        for r in range(ROWS) for c in range(COLS)
    ]


def slot_of(shape):
    return lax.broadcasted_iota(jnp.int32, shape, 1) // HALF


def crossed(load, i, group):
    slot = slot_of((32, 128))
    out = None
    for s in range(4):
        piece = load(4 * group + s, i // 4)
        shift = (s - i % 4) % 4
        if shift:
            piece = pltpu.roll(piece, shift * HALF, 1)
        out = piece if out is None else jnp.where(slot == s, piece, out)
    return out


def full_tiles():
    return [(i, g) for i in range(OCC) for g in range(i // 4 + 1, GROUPS)]


def pack_w_kernel(w_ref, w_out):
    for g in range(GROUPS):
        block = [w_ref[4 * g + s].astype(jnp.float32) for s in range(4)]
        for half in range(2):
            cut = jnp.concatenate([b[:, HALF * half : HALF * half + HALF] for b in block], axis=1)
            lane = half * SIDE + 128 * g
            w_out[:, lane : lane + 128] = cut.astype(jnp.bfloat16)


def pack_a_kernel(a_ref, a_out):
    for i in range(OCC // 2):
        a_out[32 * i : 32 * i + 32, :] = jnp.concatenate([a_ref[i], a_ref[i + 6]], axis=1)


def pack(kernel, shape, name, array):
    return pl.pallas_call(
        kernel,
        out_shape=bf16(*shape),
        in_specs=[VMEM],
        out_specs=VMEM,
        compiler_params=PARAMS,
        name=name,
    )(array)


def spread_kernel(first, count, *refs):
    blocks, out, sem = refs[-count - 2 : -2], refs[-2], refs[-1]
    copies = [
        pltpu.make_async_copy(blocks[k], out.at[x, first + k], sem.at[count * x + k])
        for x in range(X) for k in range(count)
    ]
    for copy in copies:
        copy.start()
    for copy in copies:
        copy.wait()


def spread(first, blocks, begun, name):
    count = len(blocks)
    return pl.pallas_call(
        functools.partial(spread_kernel, first, count),
        out_shape=bf16(X, S, *blocks[0].shape),
        in_specs=[HBM] * len(begun) + [VMEM] * count,
        out_specs=HBM,
        scratch_shapes=[pltpu.SemaphoreType.DMA((count * X,))],
        input_output_aliases={0: 0} if begun else {},
        compiler_params=PARAMS,
        name=name,
    )(*begun, *blocks)


def keys_kernel(place_ref, occ_ref, virt_ref, row_key, col_key, order):
    r, c = place_ref[5], place_ref[6]

    def cut(first):
        line = jnp.broadcast_to(virt_ref[pl.ds(first // 128, 1), :], (8, 128))
        return pltpu.roll(line, lax.rem(128 - lax.rem(first, 128), 128), 1)

    down = jnp.broadcast_to(cut(WA * r)[:1], (128, 128)).T[:32]
    for i in range(OCC):
        row_key[32 * i : 32 * i + 32, :] = down ^ occ_ref[i]
    slot = slot_of((8, 128))
    for half in range(2):
        line = cut(WB * c + HALF * half)
        wide = line
        for s in range(1, 4):
            wide = jnp.where(slot == s, pltpu.roll(line, s * HALF, 1), wide)
        for g in range(GROUPS):
            label = jnp.full((8, 128), occ_ref[4 * g], jnp.int32)
            for s in range(1, 4):
                label = jnp.where(slot == s, occ_ref[4 * g + s], label)
            col_key[half : half + 1, 128 * g : 128 * g + 128] = (wide ^ label)[:1]
    source = lax.broadcasted_iota(jnp.int32, (SIDE, SIDE), 0)
    target = lax.broadcasted_iota(jnp.int32, (SIDE, SIDE), 1)
    hit = (source % HALF) * OCC + source // HALF == target
    order[...] = jnp.where(hit, 1.0, 0.0).astype(jnp.bfloat16)


def keys(place, occupied_irrep, virtual_irrep):
    return pl.pallas_call(
        keys_kernel,
        out_shape=(
            jax.ShapeDtypeStruct((SIDE, 128), jnp.int32),
            jax.ShapeDtypeStruct((2, SIDE), jnp.int32),
            bf16(SIDE, SIDE),
        ),
        in_specs=[SMEM, SMEM, VMEM],
        out_specs=(VMEM, VMEM, VMEM),
        compiler_params=PARAMS,
        name="keys",
    )(place, occupied_irrep, virtual_irrep.reshape(8, 128))


def paired_half(half, lhs, w_ref, paired_ref, send_ref, prod, turned):
    lanes = pl.ds(pl.multiple_of(half * SIDE, 128), SIDE)
    prod[...] = jnp.dot(
        jnp.concatenate([lhs[p] for p in range(Q * S)], axis=1),
        jnp.concatenate([w_ref[x, k, q, :, lanes] for k in range(S) for q in range(Q) for x in range(X)], axis=0),
        preferred_element_type=jnp.float32,
    )

    def load(j, group):
        return prod[32 * j : 32 * j + 32, 128 * group : 128 * group + 128]

    for i in range(OCC):
        for g in range(GROUPS):
            paired_ref[32 * i : 32 * i + 32, 128 * g : 128 * g + 128] = (
                load(i, g) - crossed(load, i, g)
            ).astype(jnp.bfloat16)
    for block in range(GROUPS):
        for g in range(block + 1):
            down, across = slice(128 * block, 128 * block + 128), slice(128 * g, 128 * g + 128)
            turned[across, down] = paired_ref[down, across].astype(jnp.float32).T

    def tile(i, group):
        return turned[32 * i : 32 * i + 32, 128 * group : 128 * group + 128]

    slot = slot_of((32, 128))
    out = [tile(i, g) for i, g in full_tiles()]
    for q in range(GROUPS):
        out.append(jnp.where(slot == 0, pltpu.roll(tile(4 * q + 2, q), HALF, 1), tile(4 * q, q)))
    out.append(jnp.where(slot < 2, pltpu.roll(tile(5, 1), 2 * HALF, 1), tile(1, 0)))
    for t, value in enumerate(out):
        send_ref[32 * t : 32 * t + 32, :] = value.astype(jnp.bfloat16)
    rest = tile(9, 2)
    rest = jnp.where(slot[:16] < 2, pltpu.roll(rest[16:], 2 * HALF, 1), rest[:16])
    send_ref[SENT - 16 :, :] = rest.astype(jnp.bfloat16)


def first_kernel(place_ref, own_ref, far_ref, w_ref, lhs, paired_ref, send_ref, prod, turned):
    core, y, q_own, s_own = place_ref[1], place_ref[2], place_ref[3], place_ref[4]
    for step in range(Y):
        shift = lax.rem(s_own + S - jnp.bitwise_xor(y, step), S)
        k = jnp.bitwise_xor(shift, shift // 2)
        for h in range(H):
            mine, other = own_ref[step, h], far_ref[step, h]
            first = jnp.where(core == 0, mine, other)
            second = jnp.where(core == 0, other, mine)
            at = Q * k + jnp.bitwise_xor(q_own, h)
            lhs[at, :192] = jnp.concatenate([first[:, :64], second[:, :64]], axis=1)
            lhs[at, 192:] = jnp.concatenate([first[:, 64:], second[:, 64:]], axis=1)
    paired_half(place_ref[0], lhs, w_ref, paired_ref, send_ref, prod, turned)


def second_kernel(place_ref, lhs, w_ref, paired_ref, send_ref, prod, turned):
    paired_half(1 - place_ref[0], lhs, w_ref, paired_ref, send_ref, prod, turned)


WORK = [pltpu.VMEM((SIDE, SIDE), jnp.float32), pltpu.VMEM((SIDE, SIDE), jnp.float32)]


def pair_first(place, a_mine, a_other, w_all):
    return pl.pallas_call(
        first_kernel,
        out_shape=(bf16(Q * S, SIDE, 128), bf16(SIDE, SIDE), bf16(SENT, 128)),
        in_specs=[SMEM, VMEM, VMEM, VMEM],
        out_specs=(VMEM, VMEM, VMEM),
        scratch_shapes=WORK,
        compiler_params=PARAMS,
        name="pair_first",
    )(place, a_mine, a_other, w_all)


def pair_second(place, lhs, w_all):
    return pl.pallas_call(
        second_kernel,
        out_shape=(bf16(SIDE, SIDE), bf16(SENT, 128)),
        in_specs=[SMEM, VMEM, VMEM],
        out_specs=(VMEM, VMEM),
        scratch_shapes=WORK,
        compiler_params=PARAMS,
        name="pair_second",
    )(place, lhs, w_all)


def residual_half(half, paired_ref, get_ref, row_key, col_key, order, upper, whole):
    slot = slot_of((32, 128))

    def got(t):
        return get_ref[32 * t : 32 * t + 32, :].astype(jnp.float32)

    def put(i, group, mirrored, floor):
        rows, lanes = slice(32 * i, 32 * i + 32), slice(128 * group, 128 * group + 128)
        diff = paired_ref[rows, lanes].astype(jnp.float32) + mirrored
        if floor >= 0:
            diff = jnp.where(slot > floor, diff, 0.0)
        upper[rows, lanes] = diff

    for t, (i, g) in enumerate(full_tiles()):
        put(i, g, got(t), -1)
    rest = get_ref[SENT - 16 :, :].astype(jnp.float32)
    last = [got(15), jnp.concatenate([rest, pltpu.roll(rest, 2 * HALF, 1)], axis=0)]
    for q in range(GROUPS):
        piece = got(12 + q)
        put(4 * q, q, piece, 0)
        put(4 * q + 2, q, pltpu.roll(piece, 3 * HALF, 1), 2)
        put(4 * q + 1, q, (last[0], pltpu.roll(last[0], 2 * HALF, 1), last[1])[q], 1)
        upper[32 * (4 * q + 3) : 32 * (4 * q + 4), 128 * q : 128 * q + 128] = jnp.zeros((32, 128), jnp.float32)

    def load(j, group):
        return upper[32 * j : 32 * j + 32, 128 * group : 128 * group + 128]

    col = jnp.where(half == 0, col_key[0:1, :], col_key[1:2, :])
    for part in PARTS:
        for i in range(part.start // 32, part.stop // 32):
            rows = slice(32 * i, 32 * i + 32)
            for g in range(GROUPS):
                lanes = slice(128 * g, 128 * g + 128)
                if g > i // 4:
                    value = load(i, g)
                elif g < i // 4:
                    value = -crossed(load, i, g)
                else:
                    value = load(i, g) - crossed(load, i, g)
                allowed = row_key[rows, :] == col[:, lanes]
                whole[rows, lanes] = jnp.where(allowed, value, 0.0).astype(jnp.bfloat16)
        yield part, jnp.dot(whole[part, :], order[...], preferred_element_type=jnp.float32).astype(jnp.bfloat16)


def half_lanes(half):
    return pl.ds(pl.multiple_of(half * SIDE, 128), SIDE)


def finish_first_kernel(place_ref, paired_ref, get_ref, row_key, col_key, order, done_ref, upper, whole):
    for rows, value in residual_half(place_ref[0], paired_ref, get_ref, row_key, col_key, order, upper, whole):
        done_ref[rows, :] = value


def finish_second_kernel(
    place_ref, done_ref, paired_ref, get_ref, row_key, col_key, order, out_ref, upper, whole, result, sem
):
    half = place_ref[0]
    copies = [pltpu.make_async_copy(done_ref, out_ref.at[:, half_lanes(half)], sem.at[len(PARTS)])]
    copies[0].start()
    for rows, value in residual_half(1 - half, paired_ref, get_ref, row_key, col_key, order, upper, whole):
        result[rows, :] = value
        copies.append(
            pltpu.make_async_copy(result.at[rows], out_ref.at[rows, half_lanes(1 - half)], sem.at[len(copies) - 1])
        )
        copies[-1].start()
    for copy in copies:
        copy.wait()


def finish(kernel, width, out_space, scratch, name, place, *arrays):
    return pl.pallas_call(
        kernel,
        out_shape=bf16(SIDE, width),
        in_specs=[SMEM] + [VMEM] * len(arrays),
        out_specs=out_space,
        scratch_shapes=[pltpu.VMEM((SIDE, SIDE), jnp.float32), pltpu.VMEM((SIDE, SIDE), jnp.bfloat16)] + scratch,
        compiler_params=PARAMS,
        name=name,
    )(place, *arrays)


def on_device(amplitudes, cycle_vertex, occupied_irrep, virtual_irrep):
    r, c = lax.axis_index("row"), lax.axis_index("col")
    place = jnp.stack([r % 2, c % 2, c // 2 % Y, r // (S * X), r // X % S, r, c]).astype(jnp.int32)
    w_own = pack(pack_w_kernel, (32, 2 * SIDE), "pack_w", cycle_vertex)
    a_own = pack(pack_a_kernel, (192, 128), "pack_a", amplitudes)
    a_far = lax.ppermute(a_own, "col", h_swap())
    w_far = lax.ppermute(w_own, "row", q_swap())
    low = c < Y * CORE
    a_two = jnp.stack([jnp.where(low, a_own, a_far), jnp.where(low, a_far, a_own)])
    w_two = jnp.stack([w_own, w_far])
    w_s = [lax.ppermute(w_two, "row", s_shift(k)) for k in STEPS[1:]]
    w_s[0], a_two = lax.optimization_barrier((w_s[0], a_two))
    a_next = lax.ppermute(a_two, "col", y_swap(1))
    w_wide = spread(0, [w_two] + w_s[:2], (), "spread_first")
    w_s, w_wide, a_two, a_next = lax.optimization_barrier((w_s, w_wide, a_two, a_next))
    w_wide = spread(S - 1, w_s[2:], (w_wide,), "spread_last")
    w_all = lax.all_to_all(w_wide, "row", 0, 0, tiled=True, axis_index_groups=x_groups())
    a_mine = jnp.stack([a_two, a_next] + [lax.ppermute(a_two, "col", y_swap(k)) for k in (2, 3)])
    a_other = lax.ppermute(a_mine, "col", core_swap())
    row_key, col_key, order = keys(place, occupied_irrep, virtual_irrep)
    lhs, paired0, send0 = pair_first(place, a_mine, a_other, w_all)
    get0 = lax.ppermute(send0, ("row", "col"), mirror_perm(0))
    paired1, send1 = pair_second(place, lhs, w_all)
    get1 = lax.ppermute(send1, ("row", "col"), mirror_perm(1))
    keep = (row_key, col_key, order)
    done = finish(finish_first_kernel, SIDE, VMEM, [], "finish_first", place, paired0, get0, *keep)
    last = [pltpu.VMEM((SIDE, SIDE), jnp.bfloat16), pltpu.SemaphoreType.DMA((len(PARTS) + 1,))]
    result = finish(
        finish_second_kernel, 2 * SIDE, HBM, last, "finish_second", place, done, paired1, get1, *keep
    )
    return result.reshape(OCC, WA, WB * OCC)


def solution(mesh):
    return jax.shard_map(
        on_device,
        mesh=mesh,
        in_specs=(P(None, "row", "col"), P(None, "row", "col"), P(), P()),
        out_specs=P(None, "row", "col"),
        check_vma=False,
    )
```

```python
import functools

import jax
import jax.numpy as jnp
from jax import lax
from jax.experimental import pallas as pl
from jax.experimental.pallas import tpu as pltpu
from jax.sharding import PartitionSpec as P

Q, S, X = 2, 4, 4
H, Y, CORE = 2, 4, 2
ROWS, COLS = Q * S * X, H * Y * CORE
OCC, WA, WB = 12, 32, 64
HALF = 32
GROUPS = OCC // 4
SIDE = OCC * 32
SENT = 16 * 32 + 16
STEPS = (0, 1, 3, 2)
PARTS = [slice(r, r + 96) for r in range(0, SIDE, 96)]
VMEM = pl.BlockSpec(memory_space=pltpu.VMEM)
SMEM = pl.BlockSpec(memory_space=pltpu.SMEM)
HBM = pl.BlockSpec(memory_space=pltpu.HBM)
PARAMS = pltpu.CompilerParams(vmem_limit_bytes=48 * 1024 * 1024)


def bf16(*shape):
    return jax.ShapeDtypeStruct(shape, jnp.bfloat16)


def s_shift(step):
    return [(r, r // 16 * 16 + (r // X % S + step) % S * X + r % X) for r in range(ROWS)]


def q_swap():
    return [(r, r ^ (S * X)) for r in range(ROWS)]


def x_groups():
    return [[z * X + x for x in range(X)] for z in range(Q * S)]


def h_swap():
    return [(c, c ^ (Y * CORE)) for c in range(COLS)]


def y_swap(step):
    return [(c, c ^ (CORE * step)) for c in range(COLS)]


def core_swap():
    return [(c, c ^ 1) for c in range(COLS)]


def mirror_perm(step):
    return [
        (r * COLS + c, (2 * c + (step + r) % 2) * COLS + r // 2)
        for r in range(ROWS) for c in range(COLS)
    ]


def slot_of(shape):
    return lax.broadcasted_iota(jnp.int32, shape, 1) // HALF


def crossed(load, i, group):
    slot = slot_of((32, 128))
    out = None
    for s in range(4):
        piece = load(4 * group + s, i // 4)
        shift = (s - i % 4) % 4
        if shift:
            piece = pltpu.roll(piece, shift * HALF, 1)
        out = piece if out is None else jnp.where(slot == s, piece, out)
    return out


def full_tiles():
    return [(i, g) for i in range(OCC) for g in range(i // 4 + 1, GROUPS)]


def pack_w_kernel(w_ref, w_out):
    for g in range(GROUPS):
        block = [w_ref[4 * g + s].astype(jnp.float32) for s in range(4)]
        for half in range(2):
            cut = jnp.concatenate([b[:, HALF * half : HALF * half + HALF] for b in block], axis=1)
            lane = half * SIDE + 128 * g
            w_out[:, lane : lane + 128] = cut.astype(jnp.bfloat16)


def pack_a_kernel(a_ref, a_out):
    for i in range(OCC // 2):
        a_out[32 * i : 32 * i + 32, :] = jnp.concatenate([a_ref[i], a_ref[i + 6]], axis=1)


def pack(kernel, shape, name, array):
    return pl.pallas_call(
        kernel,
        out_shape=bf16(*shape),
        in_specs=[VMEM],
        out_specs=VMEM,
        compiler_params=PARAMS,
        name=name,
    )(array)


def spread_kernel(first, count, *refs):
    blocks, out, sem = refs[-count - 2 : -2], refs[-2], refs[-1]
    copies = [
        pltpu.make_async_copy(blocks[k], out.at[x, first + k], sem.at[count * x + k])
        for x in range(X) for k in range(count)
    ]
    for copy in copies:
        copy.start()
    for copy in copies:
        copy.wait()


def spread(first, blocks, begun, name):
    count = len(blocks)
    return pl.pallas_call(
        functools.partial(spread_kernel, first, count),
        out_shape=bf16(X, S, *blocks[0].shape),
        in_specs=[HBM] * len(begun) + [VMEM] * count,
        out_specs=HBM,
        scratch_shapes=[pltpu.SemaphoreType.DMA((count * X,))],
        input_output_aliases={0: 0} if begun else {},
        compiler_params=PARAMS,
        name=name,
    )(*begun, *blocks)


def keys_kernel(place_ref, occ_ref, virt_ref, row_key, col_key, order):
    r, c = place_ref[5], place_ref[6]

    def cut(first):
        line = jnp.broadcast_to(virt_ref[pl.ds(first // 128, 1), :], (8, 128))
        return pltpu.roll(line, lax.rem(128 - lax.rem(first, 128), 128), 1)

    down = jnp.broadcast_to(cut(WA * r)[:1], (128, 128)).T[:32]
    for i in range(OCC):
        row_key[32 * i : 32 * i + 32, :] = down ^ occ_ref[i]
    slot = slot_of((8, 128))
    for half in range(2):
        line = cut(WB * c + HALF * half)
        wide = line
        for s in range(1, 4):
            wide = jnp.where(slot == s, pltpu.roll(line, s * HALF, 1), wide)
        for g in range(GROUPS):
            label = jnp.full((8, 128), occ_ref[4 * g], jnp.int32)
            for s in range(1, 4):
                label = jnp.where(slot == s, occ_ref[4 * g + s], label)
            col_key[half : half + 1, 128 * g : 128 * g + 128] = (wide ^ label)[:1]
    source = lax.broadcasted_iota(jnp.int32, (SIDE, SIDE), 0)
    target = lax.broadcasted_iota(jnp.int32, (SIDE, SIDE), 1)
    hit = (source % HALF) * OCC + source // HALF == target
    order[...] = jnp.where(hit, 1.0, 0.0).astype(jnp.bfloat16)


def keys(place, occupied_irrep, virtual_irrep):
    return pl.pallas_call(
        keys_kernel,
        out_shape=(
            jax.ShapeDtypeStruct((SIDE, 128), jnp.int32),
            jax.ShapeDtypeStruct((2, SIDE), jnp.int32),
            bf16(SIDE, SIDE),
        ),
        in_specs=[SMEM, SMEM, VMEM],
        out_specs=(VMEM, VMEM, VMEM),
        compiler_params=PARAMS,
        name="keys",
    )(place, occupied_irrep, virtual_irrep.reshape(8, 128))


def paired_half(half, lhs, w_ref, paired_ref, send_ref, prod, turned):
    lanes = pl.ds(pl.multiple_of(half * SIDE, 128), SIDE)
    prod[...] = jnp.dot(
        jnp.concatenate([lhs[p] for p in range(Q * S)], axis=1),
        jnp.concatenate([w_ref[x, k, q, :, lanes] for k in range(S) for q in range(Q) for x in range(X)], axis=0),
        preferred_element_type=jnp.float32,
    )

    def load(j, group):
        return prod[32 * j : 32 * j + 32, 128 * group : 128 * group + 128]

    for i in range(OCC):
        for g in range(GROUPS):
            paired_ref[32 * i : 32 * i + 32, 128 * g : 128 * g + 128] = (
                load(i, g) - crossed(load, i, g)
            ).astype(jnp.bfloat16)
    turned[...] = paired_ref[...].astype(jnp.float32).T

    def tile(i, group):
        return turned[32 * i : 32 * i + 32, 128 * group : 128 * group + 128]

    slot = slot_of((32, 128))
    out = [tile(i, g) for i, g in full_tiles()]
    for q in range(GROUPS):
        out.append(jnp.where(slot == 0, pltpu.roll(tile(4 * q + 2, q), HALF, 1), tile(4 * q, q)))
    out.append(jnp.where(slot < 2, pltpu.roll(tile(5, 1), 2 * HALF, 1), tile(1, 0)))
    for t, value in enumerate(out):
        send_ref[32 * t : 32 * t + 32, :] = value.astype(jnp.bfloat16)
    rest = tile(9, 2)
    rest = jnp.where(slot[:16] < 2, pltpu.roll(rest[16:], 2 * HALF, 1), rest[:16])
    send_ref[SENT - 16 :, :] = rest.astype(jnp.bfloat16)


def first_kernel(place_ref, own_ref, far_ref, w_ref, lhs, paired_ref, send_ref, prod, turned):
    core, y, q_own, s_own = place_ref[1], place_ref[2], place_ref[3], place_ref[4]
    for step in range(Y):
        shift = lax.rem(s_own + S - jnp.bitwise_xor(y, step), S)
        k = jnp.bitwise_xor(shift, shift // 2)
        for h in range(H):
            mine, other = own_ref[step, h], far_ref[step, h]
            first = jnp.where(core == 0, mine, other)
            second = jnp.where(core == 0, other, mine)
            at = Q * k + jnp.bitwise_xor(q_own, h)
            lhs[at, :192] = jnp.concatenate([first[:, :64], second[:, :64]], axis=1)
            lhs[at, 192:] = jnp.concatenate([first[:, 64:], second[:, 64:]], axis=1)
    paired_half(place_ref[0], lhs, w_ref, paired_ref, send_ref, prod, turned)


def second_kernel(place_ref, lhs, w_ref, paired_ref, send_ref, prod, turned):
    paired_half(1 - place_ref[0], lhs, w_ref, paired_ref, send_ref, prod, turned)


WORK = [pltpu.VMEM((SIDE, SIDE), jnp.float32), pltpu.VMEM((SIDE, SIDE), jnp.float32)]


def pair_first(place, a_mine, a_other, w_all):
    return pl.pallas_call(
        first_kernel,
        out_shape=(bf16(Q * S, SIDE, 128), bf16(SIDE, SIDE), bf16(SENT, 128)),
        in_specs=[SMEM, VMEM, VMEM, VMEM],
        out_specs=(VMEM, VMEM, VMEM),
        scratch_shapes=WORK,
        compiler_params=PARAMS,
        name="pair_first",
    )(place, a_mine, a_other, w_all)


def pair_second(place, lhs, w_all):
    return pl.pallas_call(
        second_kernel,
        out_shape=(bf16(SIDE, SIDE), bf16(SENT, 128)),
        in_specs=[SMEM, VMEM, VMEM],
        out_specs=(VMEM, VMEM),
        scratch_shapes=WORK,
        compiler_params=PARAMS,
        name="pair_second",
    )(place, lhs, w_all)


def residual_half(half, paired_ref, get_ref, row_key, col_key, order, upper, whole):
    slot = slot_of((32, 128))

    def got(t):
        return get_ref[32 * t : 32 * t + 32, :].astype(jnp.float32)

    def put(i, group, mirrored, floor):
        rows, lanes = slice(32 * i, 32 * i + 32), slice(128 * group, 128 * group + 128)
        diff = paired_ref[rows, lanes].astype(jnp.float32) + mirrored
        if floor >= 0:
            diff = jnp.where(slot > floor, diff, 0.0)
        upper[rows, lanes] = diff

    for t, (i, g) in enumerate(full_tiles()):
        put(i, g, got(t), -1)
    rest = get_ref[SENT - 16 :, :].astype(jnp.float32)
    last = [got(15), jnp.concatenate([rest, pltpu.roll(rest, 2 * HALF, 1)], axis=0)]
    for q in range(GROUPS):
        piece = got(12 + q)
        put(4 * q, q, piece, 0)
        put(4 * q + 2, q, pltpu.roll(piece, 3 * HALF, 1), 2)
        put(4 * q + 1, q, (last[0], pltpu.roll(last[0], 2 * HALF, 1), last[1])[q], 1)
        upper[32 * (4 * q + 3) : 32 * (4 * q + 4), 128 * q : 128 * q + 128] = jnp.zeros((32, 128), jnp.float32)

    def load(j, group):
        return upper[32 * j : 32 * j + 32, 128 * group : 128 * group + 128]

    col = jnp.where(half == 0, col_key[0:1, :], col_key[1:2, :])
    for i in range(OCC):
        rows = slice(32 * i, 32 * i + 32)
        for g in range(GROUPS):
            lanes = slice(128 * g, 128 * g + 128)
            if g > i // 4:
                value = load(i, g)
            elif g < i // 4:
                value = -crossed(load, i, g)
            else:
                value = load(i, g) - crossed(load, i, g)
            allowed = row_key[rows, :] == col[:, lanes]
            whole[rows, lanes] = jnp.where(allowed, value, 0.0).astype(jnp.bfloat16)
    for rows in PARTS:
        yield rows, jnp.dot(whole[rows, :], order[...], preferred_element_type=jnp.float32).astype(jnp.bfloat16)


def half_lanes(half):
    return pl.ds(pl.multiple_of(half * SIDE, 128), SIDE)


def finish_first_kernel(place_ref, paired_ref, get_ref, row_key, col_key, order, done_ref, upper, whole):
    for rows, value in residual_half(place_ref[0], paired_ref, get_ref, row_key, col_key, order, upper, whole):
        done_ref[rows, :] = value


def finish_second_kernel(
    place_ref, done_ref, paired_ref, get_ref, row_key, col_key, order, out_ref, upper, whole, result, sem
):
    half = place_ref[0]
    copies = [pltpu.make_async_copy(done_ref, out_ref.at[:, half_lanes(half)], sem.at[len(PARTS)])]
    copies[0].start()
    for rows, value in residual_half(1 - half, paired_ref, get_ref, row_key, col_key, order, upper, whole):
        result[rows, :] = value
        copies.append(
            pltpu.make_async_copy(result.at[rows], out_ref.at[rows, half_lanes(1 - half)], sem.at[len(copies) - 1])
        )
        copies[-1].start()
    for copy in copies:
        copy.wait()


def finish(kernel, width, out_space, scratch, name, place, *arrays):
    return pl.pallas_call(
        kernel,
        out_shape=bf16(SIDE, width),
        in_specs=[SMEM] + [VMEM] * len(arrays),
        out_specs=out_space,
        scratch_shapes=[pltpu.VMEM((SIDE, SIDE), jnp.float32), pltpu.VMEM((SIDE, SIDE), jnp.bfloat16)] + scratch,
        compiler_params=PARAMS,
        name=name,
    )(place, *arrays)


def on_device(amplitudes, cycle_vertex, occupied_irrep, virtual_irrep):
    r, c = lax.axis_index("row"), lax.axis_index("col")
    place = jnp.stack([r % 2, c % 2, c // 2 % Y, r // (S * X), r // X % S, r, c]).astype(jnp.int32)
    w_own = pack(pack_w_kernel, (32, 2 * SIDE), "pack_w", cycle_vertex)
    a_own = pack(pack_a_kernel, (192, 128), "pack_a", amplitudes)
    a_far = lax.ppermute(a_own, "col", h_swap())
    w_far = lax.ppermute(w_own, "row", q_swap())
    low = c < Y * CORE
    a_two = jnp.stack([jnp.where(low, a_own, a_far), jnp.where(low, a_far, a_own)])
    w_two = jnp.stack([w_own, w_far])
    w_s = [lax.ppermute(w_two, "row", s_shift(k)) for k in STEPS[1:]]
    w_s[0], a_two = lax.optimization_barrier((w_s[0], a_two))
    a_next = lax.ppermute(a_two, "col", y_swap(1))
    w_wide = spread(0, [w_two] + w_s[:2], (), "spread_first")
    w_s, w_wide, a_two, a_next = lax.optimization_barrier((w_s, w_wide, a_two, a_next))
    w_wide = spread(S - 1, w_s[2:], (w_wide,), "spread_last")
    w_all = lax.all_to_all(w_wide, "row", 0, 0, tiled=True, axis_index_groups=x_groups())
    a_mine = jnp.stack([a_two, a_next] + [lax.ppermute(a_two, "col", y_swap(k)) for k in (2, 3)])
    a_other = lax.ppermute(a_mine, "col", core_swap())
    row_key, col_key, order = keys(place, occupied_irrep, virtual_irrep)
    lhs, paired0, send0 = pair_first(place, a_mine, a_other, w_all)
    get0 = lax.ppermute(send0, ("row", "col"), mirror_perm(0))
    paired1, send1 = pair_second(place, lhs, w_all)
    get1 = lax.ppermute(send1, ("row", "col"), mirror_perm(1))
    keep = (row_key, col_key, order)
    done = finish(finish_first_kernel, SIDE, VMEM, [], "finish_first", place, paired0, get0, *keep)
    last = [pltpu.VMEM((SIDE, SIDE), jnp.bfloat16), pltpu.SemaphoreType.DMA((len(PARTS) + 1,))]
    result = finish(
        finish_second_kernel, 2 * SIDE, HBM, last, "finish_second", place, done, paired1, get1, *keep
    )
    return result.reshape(OCC, WA, WB * OCC)


def solution(mesh):
    return jax.shard_map(
        on_device,
        mesh=mesh,
        in_specs=(P(None, "row", "col"), P(None, "row", "col"), P(), P()),
        out_specs=P(None, "row", "col"),
        check_vma=False,
    )
```
